256 devices in a mesh: group: 8 (over x, z_lo), view: 8 (over z_hi, core), tok: 4 (over y).
Axes of the slice: x: 4, y: 4, z: 8 (z_hi: 4, z_lo: 2; z = z_hi * 2 + z_lo), core: 2. Of those that a mesh axis runs over, the one named last changes fastest.
Arguments:
- tokens: bfloat16 [65536, 768], P(('group', 'view', 'tok')), may hold values from -6 to 6
- self_gain: float32 [768], replicated, may hold values from 0.5 to 1.5
- self_shift: float32 [768], replicated, may hold values from -3 to 3
- query_gain: float32 [768], replicated, may hold values from 0.5 to 1.5
- query_shift: float32 [768], replicated, may hold values from -3 to 3
- memory_gain: float32 [768], replicated, may hold values from 0.5 to 1.5
- memory_shift: float32 [768], replicated, may hold values from -3 to 3
- self_query: bfloat16 [768, 768], replicated
- self_key: bfloat16 [768, 768], replicated
- self_value: bfloat16 [768, 768], replicated, may hold values from -0.21875 to 0.21875
- self_output: bfloat16 [768, 768], replicated, may hold values from -0.21875 to 0.21875
- cross_query: bfloat16 [768, 768], replicated
- cross_key: bfloat16 [768, 768], replicated
- cross_value: bfloat16 [768, 768], replicated, may hold values from -0.21875 to 0.21875
- cross_output: bfloat16 [768, 768], replicated, may hold values from -0.21875 to 0.21875
- partner: int32 [64], replicated, may hold values from 0 to 63, as said below
- camera_rows: int32 [8, 16], replicated, may hold values from 0 to 8191, as said below
Outputs:
- mixed: float32 [65536, 768], P(('group', 'view', 'tok'))
The draws below stay inside these ranges and needn't reach their ends.
Inputs may be any that keep to these rules, and one draw needn't show every extreme that they name: partner[i] is never i. `camera_rows`: the c-th row number of a group lies in c * 512 to (c + 1) * 512 - 1.
All inputs are finite; a program needn't handle non-finite values.
Results may differ from the reference program's by a relative error of at most 0.0065.
The reference program's roundings to bfloat16 on the way count: a program that leaves them out, or rounds other values in their place, can miss the bound.
Values may be sent and summed in bfloat16 or wider, within the bound.
No kernel may reach another device: no remote copies, remote signals or barrier semaphores. Data moves between devices by JAX's collectives and lax.ppermute only.
A program may use at most 128 MiB of HBM per device.

```python
import jax
import jax.numpy as jnp
from jax import lax

D = 768
HEADS = 12
HDIM = 64
CAM = 16
VIEW_TOK = 1024
VIEWS = 64
GROUPS = 8
GROUP_ROWS = 8192
TOKENS = 65536


def shared_weight(key, salt):
    sub = jax.random.fold_in(key, salt)
    return jnp.clip(jax.random.normal(sub, (D, D), jnp.float32), -6.0, 6.0) * D ** (-0.5)


def draw_tokens(key, part):
    key = jax.random.fold_in(key, 1)
    first = jax.random.fold_in(key, 0)
    base = jnp.clip(jax.random.normal(first, (TOKENS, D), jnp.float32), -6.0, 6.0)
    return base.astype(jnp.bfloat16)


def draw_self_query(key, part):
    common = shared_weight(key, 101)
    key = jax.random.fold_in(key, 21)
    own = shared_weight(key, 5)
    return (0.8 * common + 0.6 * own).astype(jnp.bfloat16)


def draw_self_key(key, part):
    key = jax.random.fold_in(key, 2)
    own = shared_weight(key, 7)
    return own.astype(jnp.bfloat16)


def draw_cross_query(key, part):
    common = shared_weight(key, 202)
    key = jax.random.fold_in(key, 22)
    own = shared_weight(key, 5)
    return (0.8 * common + 0.6 * own).astype(jnp.bfloat16)


def draw_cross_key(key, part):
    key = jax.random.fold_in(key, 3)
    own = shared_weight(key, 7)
    return own.astype(jnp.bfloat16)


def draw_partner(key, part):
    key = jax.random.fold_in(key, 11)
    first, second, third = jax.random.split(key, 3)
    order = jax.random.permutation(first, VIEWS)
    left = jax.random.randint(second, (VIEWS,), 0, VIEWS - 1)
    right = jax.random.randint(third, (VIEWS,), 0, VIEWS - 1)
    chosen = order[jnp.minimum(left, right)]
    place = jnp.arange(VIEWS)
    chosen = jnp.where(chosen == place, order[VIEWS - 1], chosen)
    chosen = jnp.where(chosen == place, (place + 1) % VIEWS, chosen)
    chosen = chosen.at[0].set(VIEWS - 1)
    chosen = chosen.at[VIEWS - 1].set(0)
    return chosen.astype(jnp.int32)


def draw_camera_rows(key, part):
    key = jax.random.fold_in(key, 13)
    stride = GROUP_ROWS // CAM
    offset = jax.random.randint(key, (GROUPS, CAM), 0, stride)
    rows = jnp.arange(CAM)[None, :] * stride + offset
    rows = rows.at[0, 0].set(0)
    rows = rows.at[0, CAM - 1].set(GROUP_ROWS - 1)
    return rows.astype(jnp.int32)


def bell_draw(stream_key, extent, width, reach, kind=jnp.bfloat16):
    return jnp.clip(width * jax.random.normal(stream_key, extent, jnp.float32), -reach, reach).astype(kind)


def setup_inputs(seed: int = 0) -> dict:
    key_of = jax.random.split(jax.random.key(seed), 18)
    return {
        "tokens": draw_tokens(jax.random.fold_in(key_of[17], 71), 0),
        "self_gain": jnp.clip(jax.random.uniform(key_of[1], (D,), jnp.float32, 0.5, 1.5), 0.5, 1.5),
        "self_shift": bell_draw(key_of[2], (D,), 0.5, 3.0, jnp.float32),
        "query_gain": jnp.clip(jax.random.uniform(key_of[3], (D,), jnp.float32, 0.5, 1.5), 0.5, 1.5),
        "query_shift": bell_draw(key_of[4], (D,), 0.5, 3.0, jnp.float32),
        "memory_gain": jnp.clip(jax.random.uniform(key_of[5], (D,), jnp.float32, 0.5, 1.5), 0.5, 1.5),
        "memory_shift": bell_draw(key_of[6], (D,), 0.5, 3.0, jnp.float32),
        "self_query": draw_self_query(jax.random.fold_in(key_of[17], 71), 0),
        "self_key": draw_self_key(jax.random.fold_in(key_of[17], 71), 0),
        "self_value": bell_draw(key_of[9], (D, D), D ** -0.5, 0.21875),
        "self_output": bell_draw(key_of[10], (D, D), D ** -0.5, 0.21875),
        "cross_query": draw_cross_query(jax.random.fold_in(key_of[17], 71), 0),
        "cross_key": draw_cross_key(jax.random.fold_in(key_of[17], 71), 0),
        "cross_value": bell_draw(key_of[13], (D, D), D ** -0.5, 0.21875),
        "cross_output": bell_draw(key_of[14], (D, D), D ** -0.5, 0.21875),
        "partner": draw_partner(jax.random.fold_in(key_of[17], 71), 0),
        "camera_rows": draw_camera_rows(jax.random.fold_in(key_of[17], 71), 0),
    }


def normalize(values, gain, shift):
    wide = values.astype(jnp.float32)
    center = lax.optimization_barrier(jnp.mean(wide, axis=-1, keepdims=True))
    spread = lax.optimization_barrier(jnp.mean((wide - center) ** 2, axis=-1, keepdims=True))
    return ((wide - center) * lax.rsqrt(spread + 1e-06) * gain + shift).astype(jnp.bfloat16)

def project(left, weight):
    return jnp.dot(left, weight, preferred_element_type=jnp.float32).astype(jnp.bfloat16)

def attend(queries, keys, values):
    qh = queries.astype(jnp.float32).reshape(queries.shape[0], HEADS, HDIM)
    kh = keys.astype(jnp.float32).reshape(keys.shape[0], HEADS, HDIM)
    vh = values.astype(jnp.float32).reshape(values.shape[0], HEADS, HDIM)
    scores = jnp.einsum('qhd,khd->hqk', qh, kh) / jnp.sqrt(jnp.float32(HDIM))
    weights = jax.nn.softmax(scores, axis=-1).astype(jnp.bfloat16).astype(jnp.float32)
    context = jnp.einsum('hqk,khd->qhd', weights, vh)
    return context.reshape(queries.shape[0], HEADS * HDIM)

def reference(tokens, self_gain, self_shift, query_gain, query_shift, memory_gain, memory_shift, self_query, self_key, self_value, self_output, cross_query, cross_key, cross_value, cross_output, partner, camera_rows):
    hidden = normalize(tokens, self_gain, self_shift)
    sq = project(hidden, self_query).reshape(VIEWS, VIEW_TOK, D)
    sk = project(hidden, self_key).reshape(VIEWS, VIEW_TOK, D)
    sv = project(hidden, self_value).reshape(VIEWS, VIEW_TOK, D)
    self_ctx = lax.map(lambda item: attend(item[0], item[1], item[2]).astype(jnp.bfloat16), (sq, sk, sv))
    cq = project(normalize(tokens, query_gain, query_shift), cross_query).reshape(VIEWS, VIEW_TOK, D)
    memory = normalize(tokens, memory_gain, memory_shift)
    ck = project(memory, cross_key).reshape(VIEWS, VIEW_TOK, D)
    cv = project(memory, cross_value).reshape(VIEWS, VIEW_TOK, D)
    grouped = tokens.reshape(GROUPS, GROUP_ROWS, D)
    cams = jnp.take_along_axis(grouped, camera_rows.astype(jnp.int32)[:, :, None], axis=1).reshape(GROUPS * CAM, D)
    cam_memory = normalize(cams, memory_gain, memory_shift)
    camk = project(cam_memory, cross_key)
    camv = project(cam_memory, cross_value)

    def cross_one(item):
        queries, other = item
        pk = lax.dynamic_index_in_dim(ck, other, 0, keepdims=False)
        pv = lax.dynamic_index_in_dim(cv, other, 0, keepdims=False)
        total = attend(queries, pk, pv) + attend(queries, camk, camv)
        return total.astype(jnp.bfloat16)
    cross_ctx = lax.map(cross_one, (cq, partner.astype(jnp.int32)))
    self_term = jnp.dot(self_ctx.reshape(TOKENS, D), self_output, preferred_element_type=jnp.float32)
    cross_term = jnp.dot(cross_ctx.reshape(TOKENS, D), cross_output, preferred_element_type=jnp.float32)
    return tokens.astype(jnp.float32) + self_term + cross_term
```

```python
import functools

import jax
import jax.numpy as jnp
from jax import lax
from jax.experimental import pallas as pl
from jax.experimental.pallas import tpu as pltpu
from jax.sharding import Mesh, PartitionSpec as P

D = 768
HDIM = 64
COLS = 256
STEPS = D // COLS
ROUTE = ("core", "zh", "zl", "x")
ROWS = 256
PIECES = 64
VIEW = 1024


def norm(wide, gain, shift):
    center = jnp.mean(wide, axis=-1, keepdims=True)
    spread = jnp.mean((wide - center) ** 2, axis=-1, keepdims=True)
    return ((wide - center) * lax.rsqrt(spread + 1e-06) * gain + shift).astype(jnp.bfloat16)


def mm(left, right):
    return lax.dot_general(left, right, (((1,), (0,)), ((), ())), preferred_element_type=jnp.float32)


def mm_nt(left, right):
    return lax.dot_general(left, right, (((1,), (1,)), ((), ())), preferred_element_type=jnp.float32)


def attend(q, k, v):
    lane = lax.broadcasted_iota(jnp.int32, q.shape, 1) // HDIM
    out = None
    for head in range(COLS // HDIM):
        mine = lane == head
        s = mm_nt(jnp.where(mine, q, jnp.zeros_like(q)), k)
        p = jnp.exp(s - jnp.max(s, axis=-1, keepdims=True))
        total = jnp.sum(p, axis=-1, keepdims=True)
        c = mm(p.astype(jnp.bfloat16), v) / total
        out = c if out is None else jnp.where(mine, c, out)
    return out


def unpack(ref):
    wide = ref[...].astype(jnp.float32).reshape(PIECES // 2, 2, 8, D // 2)
    return jnp.concatenate(
        [wide[:, 0].reshape(ROWS, D // 2), wide[:, 1].reshape(ROWS, D // 2)], axis=1
    )


def pack_kernel(pos, cams, x_ref, o_ref):
    group, view, tok = pos[0], pos[1], pos[2]
    row = cams[group, 2 * view + tok // 2] - (view * VIEW + tok * ROWS)
    x = x_ref[...]
    pick = (lax.broadcasted_iota(jnp.int32, (8, ROWS), 1) == row).astype(jnp.bfloat16)
    cam = mm(pick, x)
    sub = lax.broadcasted_iota(jnp.int32, (8, 128), 0)
    extra = jnp.zeros((8, 128), jnp.float32)
    for r in range(D // 128):
        extra = jnp.where(sub == r, cam[:, 128 * r : 128 * (r + 1)], extra)
    wide = x.astype(jnp.float32)
    left = wide[:, : D // 2].reshape(PIECES // 2, 1, 8, D // 2)
    right = wide[:, D // 2 :].reshape(PIECES // 2, 1, 8, D // 2)
    both = jnp.concatenate([left, right], axis=1).reshape(PIECES, 8, D // 2)
    o_ref[:, :, : D // 2] = both.astype(jnp.bfloat16)
    o_ref[:, :, D // 2 :] = jnp.broadcast_to(extra[None], (PIECES, 8, 128)).astype(jnp.bfloat16)


def select_kernel(partner, r_ref, o_ref, c_ref):
    for slot in range(PIECES):
        core, zh, zl, x = slot // 32, slot // 8 % 4, slot // 4 % 2, slot % 4
        p = partner[((x * 2 + zl) * 4 + zh) * 2 + core]
        src = (p % 2) * 32 + (p // 2 % 4) * 8 + (p // 8 % 2) * 4 + p // 16
        o_ref[slot] = r_ref[src, :, : D // 2]
    c_ref[...] = r_ref[:, :, D // 2 :]


def self_kernel(x0, x1, x2, x3, gain, shift, wq, wk, wv, wo, o_ref, h_ref):
    step = pl.program_id(0)

    @pl.when(step == 0)
    def _():
        for i, ref in enumerate((x0, x1, x2, x3)):
            h_ref[i * ROWS : (i + 1) * ROWS] = norm(ref[...].astype(jnp.float32), gain[...], shift[...])
        o_ref[...] = x0[...].astype(jnp.float32)

    h = h_ref[...]
    k = mm(h, wk[...]).astype(jnp.bfloat16)
    v = mm(h, wv[...]).astype(jnp.bfloat16)
    q = mm(h[:ROWS], wq[...]).astype(jnp.bfloat16) * jnp.bfloat16(0.125)
    o_ref[...] += mm(attend(q, k, v).astype(jnp.bfloat16), wo[...])


def prep_kernel(x0, cams, qgain, qshift, mgain, mshift, wq, wk, wv, q_ref, c_ref, h_ref, m_ref):
    step = pl.program_id(0)

    @pl.when(step == 0)
    def _():
        h_ref[...] = norm(x0[...].astype(jnp.float32), qgain[...], qshift[...])
        m_ref[...] = norm(cams[...].astype(jnp.float32), mgain[...], mshift[...])

    m = m_ref[...]
    k = mm(m, wk[...]).astype(jnp.bfloat16)
    v = mm(m, wv[...]).astype(jnp.bfloat16)
    q = mm(h_ref[...], wq[...]).astype(jnp.bfloat16) * jnp.bfloat16(0.125)
    q_ref[...] = q
    c_ref[...] = attend(q, k, v)


def cross_kernel(y0, y1, y2, y3, gain, shift, wk, wv, wo, q_ref, c_ref, b_ref, o_ref, m_ref):
    step = pl.program_id(0)

    @pl.when(step == 0)
    def _():
        for i, ref in enumerate((y0, y1, y2, y3)):
            m_ref[i * ROWS : (i + 1) * ROWS] = norm(unpack(ref), gain[...], shift[...])
        o_ref[...] = b_ref[...]

    m = m_ref[...]
    k = mm(m, wk[...]).astype(jnp.bfloat16)
    v = mm(m, wv[...]).astype(jnp.bfloat16)
    ctx = attend(q_ref[...], k, v) + c_ref[...]
    o_ref[...] += mm(ctx.astype(jnp.bfloat16), wo[...])


def full(shape):
    return pl.BlockSpec(shape, lambda i: (0,) * len(shape))


WCOL = pl.BlockSpec((D, COLS), lambda i: (0, i))
WROW = pl.BlockSpec((COLS, D), lambda i: (i, 0))
XCOL = pl.BlockSpec((ROWS, COLS), lambda i: (0, i))
VEC = full((1, D))
X = full((ROWS, D))
PIECE = full((PIECES, 8, D // 2))
PARAMS = pltpu.CompilerParams(
    dimension_semantics=("arbitrary",), vmem_limit_bytes=32 * 1024 * 1024
)


def cost(keys, rows_kv):
    return pl.CostEstimate(
        flops=2 * D * D * (2 * rows_kv + 2 * ROWS) + 16 * ROWS * keys * D,
        bytes_accessed=8 * D * D,
        transcendentals=ROWS * keys * 12,
    )


def call_self(x0, x1, x2, x3, *rest):
    return pl.pallas_call(
        self_kernel,
        grid=(STEPS,),
        in_specs=[X] * 4 + [VEC] * 2 + [WCOL] * 3 + [WROW],
        out_specs=X,
        out_shape=jax.ShapeDtypeStruct((ROWS, D), jnp.float32),
        scratch_shapes=[pltpu.VMEM((VIEW, D), jnp.bfloat16)],
        compiler_params=PARAMS,
        cost_estimate=cost(VIEW, VIEW),
        name="self_attention",
    )(x0, x1, x2, x3, *rest)


def call_prep(x0, cams, *rest):
    return pl.pallas_call(
        prep_kernel,
        grid=(STEPS,),
        in_specs=[X, full((128, D))] + [VEC] * 4 + [WCOL] * 3,
        out_specs=[XCOL, XCOL],
        out_shape=[
            jax.ShapeDtypeStruct((ROWS, D), jnp.bfloat16),
            jax.ShapeDtypeStruct((ROWS, D), jnp.float32),
        ],
        scratch_shapes=[pltpu.VMEM((ROWS, D), jnp.bfloat16), pltpu.VMEM((128, D), jnp.bfloat16)],
        compiler_params=PARAMS,
        cost_estimate=cost(128, 128),
        name="camera_attention",
    )(x0, cams, *rest)


def call_cross(y0, y1, y2, y3, *rest):
    return pl.pallas_call(
        cross_kernel,
        grid=(STEPS,),
        in_specs=[PIECE] * 4 + [VEC] * 2 + [WCOL] * 2 + [WROW, XCOL, XCOL, X],
        out_specs=X,
        out_shape=jax.ShapeDtypeStruct((ROWS, D), jnp.float32),
        scratch_shapes=[pltpu.VMEM((VIEW, D), jnp.bfloat16)],
        compiler_params=PARAMS,
        cost_estimate=cost(VIEW, VIEW),
        name="cross_attention",
    )(y0, y1, y2, y3, *rest)


def call_pack(pos, camera_rows, tokens):
    return pl.pallas_call(
        pack_kernel,
        grid_spec=pltpu.PrefetchScalarGridSpec(
            num_scalar_prefetch=2,
            grid=(1,),
            in_specs=[pl.BlockSpec((ROWS, D), lambda i, *_: (0, 0))],
            out_specs=pl.BlockSpec((PIECES, 8, 512), lambda i, *_: (0, 0, 0)),
        ),
        out_shape=jax.ShapeDtypeStruct((PIECES, 8, 512), jnp.bfloat16),
        name="pack_pieces",
    )(pos, camera_rows, tokens)


def call_select(partner, first):
    return pl.pallas_call(
        select_kernel,
        grid_spec=pltpu.PrefetchScalarGridSpec(
            num_scalar_prefetch=1,
            grid=(1,),
            in_specs=[pl.BlockSpec((PIECES, 8, 512), lambda i, *_: (0, 0, 0))],
            out_specs=[
                pl.BlockSpec((PIECES, 8, 384), lambda i, *_: (0, 0, 0)),
                pl.BlockSpec((PIECES, 8, 128), lambda i, *_: (0, 0, 0)),
            ],
        ),
        out_shape=[
            jax.ShapeDtypeStruct((PIECES, 8, 384), jnp.bfloat16),
            jax.ShapeDtypeStruct((PIECES, 8, 128), jnp.bfloat16),
        ],
        name="select_pieces",
    )(partner, first)


def around(value):
    return [
        lax.ppermute(value, "tok", [(i, (i + s) % 4) for i in range(4)]) for s in (1, 3, 2)
    ]


def local(
    tokens,
    self_gain,
    self_shift,
    query_gain,
    query_shift,
    memory_gain,
    memory_shift,
    self_query,
    self_key,
    self_value,
    self_output,
    cross_query,
    cross_key,
    cross_value,
    cross_output,
    partner,
    camera_rows,
):
    row = lambda v: v.reshape(1, D)
    group = lax.axis_index(("x", "zl"))
    view = lax.axis_index(("zh", "core"))
    tok = lax.axis_index("tok")
    pos = jnp.stack([group, view, tok]).astype(jnp.int32)

    packed = call_pack(pos, camera_rows, tokens)
    first = lax.all_to_all(packed, ROUTE, split_axis=0, concat_axis=0, tiled=True)
    onward, cam_own = call_select(partner, first)
    mine = lax.all_to_all(onward, ROUTE, split_axis=0, concat_axis=0, tiled=True)

    others = around(tokens)
    base = call_self(
        tokens, *others, row(self_gain), row(self_shift), self_query, self_key, self_value, self_output
    )

    cam_parts = [cam_own] + around(cam_own)
    halves = [tok // 2] + [((tok - s) % 4) // 2 for s in (1, 3, 2)]
    cams = jnp.concatenate(
        [
            sum(jnp.where(h == want, c, jnp.zeros_like(c)) for h, c in zip(halves, cam_parts))
            for want in (0, 1)
        ],
        axis=0,
    )
    cams = cams[:, :6].reshape(128, D)
    cq, cam_ctx = call_prep(
        tokens,
        cams,
        row(query_gain),
        row(query_shift),
        row(memory_gain),
        row(memory_shift),
        cross_query,
        cross_key,
        cross_value,
    )
    theirs = around(mine)
    return call_cross(
        mine,
        *theirs,
        row(memory_gain),
        row(memory_shift),
        cross_key,
        cross_value,
        cross_output,
        cq,
        cam_ctx,
        base,
    )


def solution(mesh):
    split = Mesh(mesh.devices.reshape(4, 2, 4, 2, 4), ("x", "zl", "zh", "core", "tok"))
    rows = P(("x", "zl", "zh", "core", "tok"), None)
    return jax.shard_map(
        local, mesh=split, in_specs=(rows,) + (P(),) * 16, out_specs=rows, check_vma=False
    )
```

```python
import jax
import jax.numpy as jnp
from jax import lax
from jax.experimental import pallas as pl
from jax.experimental.pallas import tpu as pltpu
from jax.sharding import Mesh, PartitionSpec as P

D = 768
HDIM = 64
COLS = 256
STEPS = D // COLS
HEADS = COLS // HDIM
ROUTE = ("core", "zh", "zl", "x")
ROWS = 256
PIECES = 64
VIEW = 1024
BF = jnp.bfloat16


def norm(wide, gain, shift):
    center = jnp.mean(wide, axis=-1, keepdims=True)
    spread = jnp.mean((wide - center) ** 2, axis=-1, keepdims=True)
    return ((wide - center) * lax.rsqrt(spread + 1e-06) * gain + shift).astype(BF)


def mm(left, right):
    return lax.dot_general(left, right, (((1,), (0,)), ((), ())), preferred_element_type=jnp.float32)


def mm_nt(left, right):
    return lax.dot_general(left, right, (((1,), (1,)), ((), ())), preferred_element_type=jnp.float32)


def heads(q, k, v):
    lane = lax.broadcasted_iota(jnp.int32, q.shape, 1) // HDIM
    score = lambda head: mm_nt(jnp.where(lane == head, q, jnp.zeros_like(q)), k)
    ahead = score(0)
    for head in range(HEADS):
        s = ahead
        if head + 1 < HEADS:
            ahead = score(head + 1)
        top = jnp.max(s, axis=-1, keepdims=True)
        p = jnp.exp(s - top)
        yield lane == head, top, jnp.sum(p, axis=-1, keepdims=True), mm(p.astype(BF), v)


def attend(q, k, v):
    out = None
    for mine, _, total, c in heads(q, k, v):
        c = c / total
        out = c if out is None else jnp.where(mine, c, out)
    return out


def heads_t(q, k, vt):
    lane = lax.broadcasted_iota(jnp.int32, q.shape, 1) // HDIM
    score = lambda head: mm_nt(k, jnp.where(lane == head, q, jnp.zeros_like(q)))
    ahead = score(0)
    for head in range(HEADS):
        s = ahead
        if head + 1 < HEADS:
            ahead = score(head + 1)
        top = jnp.max(s, axis=0, keepdims=True)
        p = jnp.exp(s - top)
        c = mm(vt[HDIM * head : HDIM * (head + 1)], p.astype(BF))
        yield slice(HDIM * head, HDIM * (head + 1)), head, top, jnp.sum(p, axis=0, keepdims=True), c


def mm_tn(left, right):
    return lax.dot_general(left, right, (((0,), (0,)), ((), ())), preferred_element_type=jnp.float32)


def project(refs, w, out):
    for i, ref in enumerate(refs):
        out[i * ROWS : (i + 1) * ROWS] = mm(ref[...], w).astype(BF)


def pack_kernel(cams, x_ref, gain, shift, o_ref):
    group = lax.axis_index(("x", "zl"))
    view = lax.axis_index(("zh", "core"))
    tok = lax.axis_index("tok")
    row = cams[group, 2 * view + tok // 2] - (view * VIEW + tok * ROWS)
    m = norm(x_ref[...].astype(jnp.float32), gain[...][None], shift[...][None])
    pick = (lax.broadcasted_iota(jnp.int32, (8, ROWS), 1) == row).astype(BF)
    cam = mm(pick, m)
    sub = lax.broadcasted_iota(jnp.int32, (8, 128), 0)
    extra = jnp.zeros((8, 128), jnp.float32)
    for c in range(D // 128):
        extra = jnp.where(sub == c, cam[:, 128 * c : 128 * (c + 1)], extra)
        tiles = m[:, 128 * c : 128 * (c + 1)].astype(jnp.float32).reshape(ROWS // 8, 8, 128)
        o_ref[:, c // 3, c % 3] = tiles.astype(BF)
    spread = jnp.broadcast_to(extra[None], (ROWS // 8, 8, 128)).astype(BF)
    o_ref[:, 0, 3] = spread
    o_ref[:, 1, 3] = spread


def norm_kernel(x_ref, gain, shift, o_ref):
    o_ref[...] = norm(x_ref[...].astype(jnp.float32), gain[...][None], shift[...][None])


def query_kernel(x_ref, h_ref, gain, shift, wc, ws, c_ref, s_ref, n_ref):
    @pl.when(pl.program_id(0) == 0)
    def _():
        n_ref[...] = norm(x_ref[...].astype(jnp.float32), gain[...][None], shift[...][None])

    c_ref[...] = mm(n_ref[...], wc[...]).astype(BF) * BF(0.125)
    s_ref[...] = mm(h_ref[...], ws[...]).astype(BF) * BF(0.125)


def self_kernel(*refs):
    sources, o_ref, held, k_ref, v_ref, c_ref, sems = refs[:9], refs[9], refs[10:19], *refs[19:23]
    copies = [
        pltpu.make_async_copy(src, dst, sems.at[i])
        for i, (src, dst) in enumerate(zip(sources, held))
    ]
    for copy in copies:
        copy.start()
    (h0, wk, h1, h2, h3, wv, q_ref, x_ref, wo) = held
    copies[0].wait()
    copies[1].wait()
    for i, h in enumerate((h0, h1, h2, h3)):
        if i:
            copies[i + 1].wait()
        k_ref[i * ROWS : (i + 1) * ROWS] = mm(h[...], wk[...]).astype(BF)
    copies[5].wait()
    for i, h in enumerate((h0, h1, h2, h3)):
        v_ref[i * ROWS : (i + 1) * ROWS] = mm(h[...], wv[...]).astype(BF)
    copies[6].wait()
    for step in range(STEPS):
        at = slice(step * COLS, (step + 1) * COLS)
        c_ref[:, at] = attend(q_ref[:, at], k_ref[:, at], v_ref[:, at]).astype(BF)
    copies[7].wait()
    copies[8].wait()
    o_ref[...] = x_ref[...].astype(jnp.float32) + mm(c_ref[...], wo[...])


def camera_kernel(p0, p1, p2, p3, q_ref, wk, wv, c_ref, m_ref):
    @pl.when(pl.program_id(0) == 0)
    def _():
        tok = lax.axis_index("tok")
        parts = [ref[...].astype(jnp.float32) for ref in (p0, p1, p2, p3)]
        for half in (0, 1):
            total = jnp.zeros((PIECES, 8, 128), jnp.float32)
            for shift, part in zip((0, 1, 3, 2), parts):
                total += jnp.where((tok + 4 - shift) % 4 // 2 == half, part, 0.0)
            for c in range(D // 128):
                m_ref[PIECES * half : PIECES * (half + 1), 128 * c : 128 * (c + 1)] = total[
                    :, c, :
                ].astype(BF)

    m = m_ref[...]
    k = mm(m, wk[...]).astype(BF)
    v = mm(m, wv[...]).astype(BF)
    for at, _, _, total, c in heads_t(q_ref[...], k, jnp.transpose(v)):
        c_ref[at] = c * (1.0 / total)


def early_kernel(m0, m1, m2, q_ref, wk, wv, c_ref, t_ref, l_ref, k_ref, v_ref):
    project((m0, m1, m2), wk[...], k_ref)
    project((m0, m1, m2), wv[...], v_ref)
    for at, head, top, total, c in heads_t(q_ref[...], k_ref[...], jnp.transpose(v_ref[...])):
        c_ref[at] = c
        t_ref[head : head + 1] = top
        l_ref[head : head + 1] = total


def late_kernel(ma, mb, q_ref, wk, wv, wo, c_ref, t_ref, l_ref, cam_ref, b_ref, o_ref):
    @pl.when(pl.program_id(0) == 0)
    def _():
        o_ref[...] = b_ref[...]

    m = jnp.concatenate([ma[...], mb[...]], axis=0)
    k = mm(m, wk[...]).astype(BF)
    v = mm(m, wv[...]).astype(BF)
    ctx = []
    for at, head, top, total, c in heads_t(q_ref[...], k, jnp.transpose(v)):
        top0 = t_ref[head : head + 1]
        best = jnp.maximum(top, top0)
        w0 = jnp.exp(top0 - best)
        w1 = jnp.exp(top - best)
        down = 1.0 / (w0 * l_ref[head : head + 1] + w1 * total)
        ctx.append(c_ref[at] * (w0 * down) + c * (w1 * down) + cam_ref[at])
    o_ref[...] += mm_tn(jnp.concatenate(ctx, axis=0).astype(BF), wo[...])


def full(shape):
    return pl.BlockSpec(shape, lambda i: (0,) * len(shape))


WCOL = pl.BlockSpec((D, COLS), lambda i: (0, i))
WROW = pl.BlockSpec((COLS, D), lambda i: (i, 0))
XCOL = pl.BlockSpec((ROWS, COLS), lambda i: (0, i))
CTX = pl.BlockSpec((COLS, ROWS), lambda i: (i, 0))
STAT = pl.BlockSpec((8, ROWS), lambda i: (i, 0))
VEC = full((D,))
X = full((ROWS, D))
HALF = full((ROWS // 2, D))
CAMS = full((PIECES, 8, 128))


def shape(*dims, dtype=BF):
    return jax.ShapeDtypeStruct(dims, dtype)


def call(name, kernel, ins, outs, out_shape, scratch=(), steps=STEPS, work=0, limit=32):
    return pl.pallas_call(
        kernel,
        grid=(steps,),
        in_specs=ins,
        out_specs=outs,
        out_shape=out_shape,
        scratch_shapes=list(scratch),
        compiler_params=pltpu.CompilerParams(
            dimension_semantics=("arbitrary",), vmem_limit_bytes=limit * 1024 * 1024
        ),
        cost_estimate=pl.CostEstimate(
            flops=work, bytes_accessed=2 * D * D * 2, transcendentals=0
        ),
        name=name,
    )


def call_pack(camera_rows, tokens, gain, shift):
    return pl.pallas_call(
        pack_kernel,
        grid_spec=pltpu.PrefetchScalarGridSpec(
            num_scalar_prefetch=1,
            grid=(1,),
            in_specs=[
                pl.BlockSpec((ROWS, D), lambda i, *_: (0, 0)),
                pl.BlockSpec((D,), lambda i, *_: (0,)),
                pl.BlockSpec((D,), lambda i, *_: (0,)),
            ],
            out_specs=pl.BlockSpec((ROWS // 8, 2, 4, 8, 128), lambda i, *_: (0, 0, 0, 0, 0)),
        ),
        out_shape=shape(ROWS // 8, 2, 4, 8, 128),
        name="memory_norm",
    )(camera_rows, tokens, gain, shift)


def call_self(*operands):
    return pl.pallas_call(
        self_kernel,
        in_specs=[pl.BlockSpec(memory_space=pl.ANY)] * 9,
        out_specs=pl.BlockSpec(memory_space=pltpu.VMEM),
        out_shape=shape(ROWS, D, dtype=jnp.float32),
        scratch_shapes=[pltpu.VMEM(v.shape, BF) for v in operands]
        + [pltpu.VMEM((VIEW, D), BF)] * 2
        + [pltpu.VMEM((ROWS, D), BF), pltpu.SemaphoreType.DMA((9,))],
        compiler_params=pltpu.CompilerParams(vmem_limit_bytes=60 * 1024 * 1024),
        cost_estimate=pl.CostEstimate(
            flops=4 * VIEW * D * D + 16 * ROWS * VIEW * D,
            bytes_accessed=10 * D * D,
            transcendentals=0,
        ),
        name="self_attention",
    )(*operands)


def to_tiles(x):
    return x.reshape(32, 8, 6, 128).transpose(0, 2, 1, 3).reshape(PIECES, 24, 128)


def from_tiles(pieces):
    return pieces.reshape(32, 6, 8, 128).transpose(0, 2, 1, 3).reshape(ROWS, D)


def turn(shift):
    return [(i, (i + shift) % 4) for i in range(4)]


def around(value):
    return [lax.ppermute(value, "tok", turn(shift)) for shift in (1, 3, 2)]


def local(
    tokens,
    self_gain,
    self_shift,
    query_gain,
    query_shift,
    memory_gain,
    memory_shift,
    self_query,
    self_key,
    self_value,
    self_output,
    cross_query,
    cross_key,
    cross_value,
    cross_output,
    partner,
    camera_rows,
):
    packed = call_pack(camera_rows, tokens, memory_gain, memory_shift).reshape(PIECES, 32, 128)
    first = lax.all_to_all(packed, ROUTE, split_axis=0, concat_axis=0, tiled=True)
    wanted = partner.reshape(4, 2, 4, 2).transpose(3, 2, 1, 0).reshape(PIECES)
    place = (wanted % 2) * 32 + (wanted // 2 % 4) * 8 + (wanted // 8 % 2) * 4 + wanted // 16
    place = (place[:, None] * 4 + jnp.arange(3)[None, :]).reshape(PIECES * 3)
    onward = first.reshape(PIECES * 4, 8, 128).at[place].get(mode="promise_in_bounds")
    onward = onward.reshape(PIECES, 24, 128)
    cam_own = first[:, 24:]

    hidden = call("self_norm", norm_kernel, [X, VEC, VEC], X, shape(ROWS, D), steps=1)(
        tokens, self_gain, self_shift
    )
    others = around(hidden)
    cq, sq = call(
        "queries",
        query_kernel,
        [X, X, VEC, VEC, WCOL, WCOL],
        [XCOL, XCOL],
        [shape(ROWS, D), shape(ROWS, D)],
        [pltpu.VMEM((ROWS, D), BF)],
        work=4 * ROWS * D * D,
    )(tokens, hidden, query_gain, query_shift, cross_query, self_query)
    sq, onward = lax.optimization_barrier((sq, onward))
    base = call_self(hidden, self_key, *others, self_value, sq, tokens, self_output)

    mine = lax.all_to_all(onward, ROUTE, split_axis=0, concat_axis=0, tiled=True)
    cam_parts = [cam_own] + around(cam_own)
    mine, base, cq, *cam_parts = lax.optimization_barrier((mine, base, cq, *cam_parts))
    mine = from_tiles(mine)
    near_a = lax.ppermute(mine, "tok", turn(1))
    near_b = lax.ppermute(mine, "tok", turn(3))
    far_a = lax.ppermute(near_a[: ROWS // 2], "tok", turn(1))
    far_b = lax.ppermute(near_b[ROWS // 2 :], "tok", turn(3))
    cam_ctx = call(
        "camera_attention",
        camera_kernel,
        [CAMS] * 4 + [XCOL, WCOL, WCOL],
        CTX,
        shape(D, ROWS, dtype=jnp.float32),
        [pltpu.VMEM((2 * PIECES, D), BF)],
        work=4 * 128 * D * D + 16 * ROWS * 128 * D,
    )(*cam_parts, cq, cross_key, cross_value)
    ctx, tops, sums = call(
        "cross_early",
        early_kernel,
        [X] * 3 + [XCOL, WCOL, WCOL],
        [CTX, STAT, STAT],
        [shape(n, ROWS, dtype=jnp.float32) for n in (D, 8 * STEPS, 8 * STEPS)],
        [pltpu.VMEM((3 * ROWS, COLS), BF)] * 2,
        work=12 * ROWS * D * D + 48 * ROWS * ROWS * D,
    )(mine, near_a, near_b, cq, cross_key, cross_value)
    return call(
        "cross_late",
        late_kernel,
        [HALF, HALF, XCOL, WCOL, WCOL, WROW, CTX, STAT, STAT, CTX, X],
        X,
        shape(ROWS, D, dtype=jnp.float32),
        work=4 * ROWS * D * D + 16 * ROWS * ROWS * D,
    )(far_a, far_b, cq, cross_key, cross_value, cross_output, ctx, tops, sums, cam_ctx, base)


def solution(mesh):
    split = Mesh(mesh.devices.reshape(4, 2, 4, 2, 4), ("x", "zl", "zh", "core", "tok"))
    rows = P(("x", "zl", "zh", "core", "tok"), None)
    return jax.shard_map(
        local, mesh=split, in_specs=(rows,) + (P(),) * 16, out_specs=rows, check_vma=False
    )
```

```python
import functools

import jax
import jax.numpy as jnp
from jax import lax
from jax.experimental import pallas as pl
from jax.experimental.pallas import tpu as pltpu
from jax.sharding import Mesh, PartitionSpec as P

D = 768
HDIM = 64
COLS = 256
STEPS = D // COLS
HEADS = COLS // HDIM
ROUTE = ("core", "zh", "zl", "x")
ROWS = 256
PIECES = 64
VIEW = 1024
BF = jnp.bfloat16


def norm(wide, gain, shift):
    center = jnp.mean(wide, axis=-1, keepdims=True)
    spread = jnp.mean((wide - center) ** 2, axis=-1, keepdims=True)
    return ((wide - center) * lax.rsqrt(spread + 1e-06) * gain + shift).astype(BF)


def mm(left, right):
    return lax.dot_general(left, right, (((1,), (0,)), ((), ())), preferred_element_type=jnp.float32)


def mm_nt(left, right):
    return lax.dot_general(left, right, (((1,), (1,)), ((), ())), preferred_element_type=jnp.float32)


def heads(q, k, v):
    lane = lax.broadcasted_iota(jnp.int32, q.shape, 1) // HDIM
    score = lambda head: mm_nt(jnp.where(lane == head, q, jnp.zeros_like(q)), k)
    ahead = score(0)
    for head in range(HEADS):
        s = ahead
        if head + 1 < HEADS:
            ahead = score(head + 1)
        top = jnp.max(s, axis=-1, keepdims=True)
        p = jnp.exp(s - top)
        yield lane == head, top, jnp.sum(p, axis=-1, keepdims=True), mm(p.astype(BF), v)


def attend(q, k, v):
    out = None
    for mine, _, total, c in heads(q, k, v):
        c = c / total
        out = c if out is None else jnp.where(mine, c, out)
    return out


def heads_t(q, k, vt):
    lane = lax.broadcasted_iota(jnp.int32, q.shape, 1) // HDIM
    score = lambda head: mm_nt(k, jnp.where(lane == head, q, jnp.zeros_like(q)))
    ahead = score(0)
    for head in range(HEADS):
        s = ahead
        if head + 1 < HEADS:
            ahead = score(head + 1)
        top = jnp.max(s, axis=0, keepdims=True)
        p = jnp.exp(s - top)
        c = mm(vt[HDIM * head : HDIM * (head + 1)], p.astype(BF))
        yield slice(HDIM * head, HDIM * (head + 1)), head, top, jnp.sum(p, axis=0, keepdims=True), c


def mm_tn(left, right):
    return lax.dot_general(left, right, (((0,), (0,)), ((), ())), preferred_element_type=jnp.float32)


def pack_kernel(cams, x_ref, gain, shift, o_ref):
    group = lax.axis_index(("x", "zl"))
    view = lax.axis_index(("zh", "core"))
    tok = lax.axis_index("tok")
    row = cams[group, 2 * view + tok // 2] - (view * VIEW + tok * ROWS)
    m = norm(x_ref[...].astype(jnp.float32), gain[...][None], shift[...][None])
    pick = (lax.broadcasted_iota(jnp.int32, (8, ROWS), 1) == row).astype(BF)
    cam = mm(pick, m)
    sub = lax.broadcasted_iota(jnp.int32, (8, 128), 0)
    extra = jnp.zeros((8, 128), jnp.float32)
    for c in range(D // 128):
        extra = jnp.where(sub == c, cam[:, 128 * c : 128 * (c + 1)], extra)
        tiles = m[:, 128 * c : 128 * (c + 1)].astype(jnp.float32).reshape(ROWS // 8, 8, 128)
        o_ref[:, c // 3, c % 3] = tiles.astype(BF)
    spread = jnp.broadcast_to(extra[None], (ROWS // 8, 8, 128)).astype(BF)
    o_ref[:, 0, 3] = spread
    o_ref[:, 1, 3] = spread


def norm_kernel(x_ref, gain, shift, o_ref):
    o_ref[...] = norm(x_ref[...].astype(jnp.float32), gain[...][None], shift[...][None])


def query_kernel(x_ref, h_ref, gain, shift, wc, ws, c_ref, s_ref, n_ref):
    @pl.when(pl.program_id(0) == 0)
    def _():
        n_ref[...] = norm(x_ref[...].astype(jnp.float32), gain[...][None], shift[...][None])

    c_ref[...] = mm(n_ref[...], wc[...]).astype(BF) * BF(0.125)
    s_ref[...] = mm(h_ref[...], ws[...]).astype(BF) * BF(0.125)


def camera_kernel(p0, p1, p2, p3, q_ref, wk, wv, c_ref, m_ref):
    @pl.when(pl.program_id(0) == 0)
    def _():
        tok = lax.axis_index("tok")
        parts = [ref[...].astype(jnp.float32) for ref in (p0, p1, p2, p3)]
        for half in (0, 1):
            total = jnp.zeros((PIECES, 8, 128), jnp.float32)
            for shift, part in zip((0, 1, 3, 2), parts):
                total += jnp.where((tok + 4 - shift) % 4 // 2 == half, part, 0.0)
            for c in range(D // 128):
                m_ref[PIECES * half : PIECES * (half + 1), 128 * c : 128 * (c + 1)] = total[
                    :, c, :
                ].astype(BF)

    m = m_ref[...]
    k = mm(m, wk[...]).astype(BF)
    v = mm(m, wv[...]).astype(BF)
    for at, _, _, total, c in heads_t(q_ref[...], k, jnp.transpose(v)):
        c_ref[at] = c * (1.0 / total)


def keys_values(blocks, wk, wv):
    m = blocks[0][...] if len(blocks) == 1 else jnp.concatenate([r[...] for r in blocks], axis=0)
    return mm(m, wk[...]).astype(BF), jnp.transpose(mm(m, wv[...]).astype(BF))


def merged(parts, state):
    c_ref, t_ref, l_ref = state
    for at, head, top, total, c in parts:
        top0 = t_ref[head : head + 1]
        best = jnp.maximum(top, top0)
        w0 = jnp.exp(top0 - best)
        w1 = jnp.exp(top - best)
        yield at, head, best, w0 * l_ref[head : head + 1] + w1 * total, c_ref[at] * w0 + c * w1


def part_kernel(blocks, *refs):
    q_ref, wk, wv, c_ref, t_ref, l_ref = refs[blocks:][-6:]
    k, vt = keys_values(refs[:blocks], wk, wv)
    parts = heads_t(q_ref[...], k, vt)
    state = refs[blocks : len(refs) - 6]
    for at, head, top, total, c in merged(parts, state) if state else parts:
        c_ref[at] = c
        t_ref[head : head + 1] = top
        l_ref[head : head + 1] = total


def last_kernel(blocks, *refs):
    *extra, q_ref, wk, wv, wo, c_ref, t_ref, l_ref, b_ref, o_ref = refs[blocks:]

    @pl.when(pl.program_id(0) == 0)
    def _():
        o_ref[...] = b_ref[...].astype(jnp.float32)

    k, vt = keys_values(refs[:blocks], wk, wv)
    ctx = []
    for at, _, _, total, c in merged(heads_t(q_ref[...], k, vt), (c_ref, t_ref, l_ref)):
        c = c * (1.0 / total)
        ctx.append(c + extra[0][at] if extra else c)
    o_ref[...] += mm_tn(jnp.concatenate(ctx, axis=0).astype(BF), wo[...])


def others_kernel(*refs):
    h1, h2, h3, wk, q, wv, c, t, l, x, wo = refs[:11]
    o_ref = refs[11]
    hb, kb, qb, vb, cb, tb, lb, xb, ob, sems = refs[12:]
    moves = {}

    def start(name, src, dst):
        moves[name] = pltpu.make_async_copy(src, dst, sems.at[len(moves)])
        moves[name].start()

    def weights(step):
        at = pl.ds(step * COLS, COLS)
        start(("k", step), wk.at[:, at], kb.at[:, at])
        start(("v", step), wv.at[:, at], vb.at[:, at])

    for i, h in enumerate((h1, h2, h3)):
        start(("h", i), h, hb.at[pl.ds(i * ROWS, ROWS)])
        if i == 0:
            weights(0)
    start("q", q, qb)
    ctx = []
    for step in range(STEPS):
        at = slice(step * COLS, (step + 1) * COLS)
        moves[("k", step)].wait()
        moves[("v", step)].wait()
        if step == 0:
            for i in range(3):
                moves[("h", i)].wait()
            moves["q"].wait()
            for name, src, dst in (("c", c, cb), ("t", t, tb), ("l", l, lb)):
                start(name, src, dst)
        if step + 1 < STEPS:
            weights(step + 1)
        if step == 1:
            start("x", x, xb)
            start("o", wo, ob)
        k = mm(hb[...], kb[:, at]).astype(BF)
        vt = jnp.transpose(mm(hb[...], vb[:, at]).astype(BF))
        parts = heads_t(qb[:, at], k, vt)
        if step == 0:
            for name in "ctl":
                moves[name].wait()
        state = (
            cb.at[pl.ds(step * COLS, COLS)],
            tb.at[pl.ds(step * 8, 8)],
            lb.at[pl.ds(step * 8, 8)],
        )
        for _, _, _, total, value in merged(parts, state):
            ctx.append((value * (1.0 / total)).astype(BF))
    moves["x"].wait()
    moves["o"].wait()
    o_ref[...] = xb[...].astype(jnp.float32) + mm_tn(jnp.concatenate(ctx, axis=0), ob[...])


def call_others(others, q, wk, wv, wo, state, tokens):
    operands = (*others, wk, q, wv, *state, tokens, wo)
    buffers = [(3 * ROWS, D), (D, D), (ROWS, D), (D, D)]
    return pl.pallas_call(
        others_kernel,
        in_specs=[pl.BlockSpec(memory_space=pl.ANY)] * len(operands),
        out_specs=pl.BlockSpec(memory_space=pltpu.VMEM),
        out_shape=shape(ROWS, D, dtype=jnp.float32),
        scratch_shapes=[pltpu.VMEM(dims, BF) for dims in buffers]
        + [pltpu.VMEM(value.shape, value.dtype) for value in (*state, tokens, wo)]
        + [pltpu.SemaphoreType.DMA((15,))],
        compiler_params=pltpu.CompilerParams(vmem_limit_bytes=60 * 1024 * 1024),
        cost_estimate=pl.CostEstimate(
            flops=12 * ROWS * D * D + 48 * ROWS * ROWS * D,
            bytes_accessed=8 * D * D,
            transcendentals=0,
        ),
        name="self_others",
    )(*operands)


def full(shape):
    return pl.BlockSpec(shape, lambda i: (0,) * len(shape))


WCOL = pl.BlockSpec((D, COLS), lambda i: (0, i))
WROW = pl.BlockSpec((COLS, D), lambda i: (i, 0))
XCOL = pl.BlockSpec((ROWS, COLS), lambda i: (0, i))
CTX = pl.BlockSpec((COLS, ROWS), lambda i: (i, 0))
STAT = pl.BlockSpec((8, ROWS), lambda i: (i, 0))
VEC = full((D,))
X = full((ROWS, D))
HALF = full((ROWS // 2, D))
CAMS = full((PIECES, 8, 128))


def shape(*dims, dtype=BF):
    return jax.ShapeDtypeStruct(dims, dtype)


def call(name, kernel, ins, outs, out_shape, scratch=(), steps=STEPS, work=0, limit=32):
    return pl.pallas_call(
        kernel,
        grid=(steps,),
        in_specs=ins,
        out_specs=outs,
        out_shape=out_shape,
        scratch_shapes=list(scratch),
        compiler_params=pltpu.CompilerParams(
            dimension_semantics=("arbitrary",), vmem_limit_bytes=limit * 1024 * 1024
        ),
        cost_estimate=pl.CostEstimate(
            flops=work, bytes_accessed=2 * D * D * 2, transcendentals=0
        ),
        name=name,
    )


def call_pack(camera_rows, tokens, gain, shift):
    vmem = pl.BlockSpec(memory_space=pltpu.VMEM)
    return pl.pallas_call(
        pack_kernel,
        in_specs=[pl.BlockSpec(memory_space=pltpu.SMEM), vmem, vmem, vmem],
        out_specs=vmem,
        out_shape=shape(ROWS // 8, 2, 4, 8, 128),
        name="memory_norm",
    )(camera_rows, tokens, gain, shift)


def call_part(name, blocks, state, *rest):
    rows = sum(b.shape[0] for b in blocks)
    return call(
        name,
        functools.partial(part_kernel, len(blocks)),
        [full(b.shape) for b in blocks] + [CTX, STAT, STAT][: len(state)] + [XCOL, WCOL, WCOL],
        [CTX, STAT, STAT],
        [shape(n, ROWS, dtype=jnp.float32) for n in (D, 8 * STEPS, 8 * STEPS)],
        work=4 * rows * D * D + 16 * rows * ROWS * D,
    )(*blocks, *state, *rest)


def call_last(name, blocks, extra, rest, state, base, limit=32):
    rows = sum(b.shape[0] for b in blocks)
    return call(
        name,
        functools.partial(last_kernel, len(blocks)),
        [full(b.shape) for b in blocks]
        + [CTX] * len(extra)
        + [XCOL, WCOL, WCOL, WROW, CTX, STAT, STAT, X],
        X,
        shape(ROWS, D, dtype=jnp.float32),
        work=4 * rows * D * D + 16 * rows * ROWS * D + 2 * ROWS * D * D,
        limit=limit,
    )(*blocks, *extra, *rest, *state, base)


def to_tiles(x):
    return x.reshape(32, 8, 6, 128).transpose(0, 2, 1, 3).reshape(PIECES, 24, 128)


def from_tiles(pieces):
    return pieces.reshape(32, 6, 8, 128).transpose(0, 2, 1, 3).reshape(ROWS, D)


def turn(shift):
    return [(i, (i + shift) % 4) for i in range(4)]


def around(value):
    return [lax.ppermute(value, "tok", turn(shift)) for shift in (1, 3, 2)]


def local(
    tokens,
    self_gain,
    self_shift,
    query_gain,
    query_shift,
    memory_gain,
    memory_shift,
    self_query,
    self_key,
    self_value,
    self_output,
    cross_query,
    cross_key,
    cross_value,
    cross_output,
    partner,
    camera_rows,
):
    packed = call_pack(camera_rows, tokens, memory_gain, memory_shift).reshape(PIECES, 32, 128)
    first = lax.all_to_all(packed, ROUTE, split_axis=0, concat_axis=0, tiled=True)
    wanted = partner.reshape(4, 2, 4, 2).transpose(3, 2, 1, 0).reshape(PIECES)
    place = (wanted % 2) * 32 + (wanted // 2 % 4) * 8 + (wanted // 8 % 2) * 4 + wanted // 16
    place = (place[:, None] * 4 + jnp.arange(3)[None, :]).reshape(PIECES * 3)
    onward = first.reshape(PIECES * 4, 8, 128).at[place].get(mode="promise_in_bounds")
    onward = onward.reshape(PIECES, 24, 128)
    cam_own = first[:, 24:]

    hidden = call("self_norm", norm_kernel, [X, VEC, VEC], X, shape(ROWS, D), steps=1)(
        tokens, self_gain, self_shift
    )
    others = around(hidden)
    cq, sq = call(
        "queries",
        query_kernel,
        [X, X, VEC, VEC, WCOL, WCOL],
        [XCOL, XCOL],
        [shape(ROWS, D), shape(ROWS, D)],
        [pltpu.VMEM((ROWS, D), BF)],
        work=4 * ROWS * D * D,
    )(tokens, hidden, query_gain, query_shift, cross_query, self_query)
    self_state = call_part("self_own", [hidden], [], sq, self_key, self_value)
    *self_state, onward = lax.optimization_barrier((*self_state, onward))
    base = call_others(
        others, sq, self_key, self_value, self_output, self_state, tokens
    )

    mine = lax.all_to_all(onward, ROUTE, split_axis=0, concat_axis=0, tiled=True)
    cam_parts = [cam_own] + around(cam_own)
    mine, base, *cam_parts[1:] = lax.optimization_barrier((mine, base, *cam_parts[1:]))
    mine = from_tiles(mine)
    near_a = lax.ppermute(mine, "tok", turn(1))
    near_b = lax.ppermute(mine, "tok", turn(3))
    far_a = lax.ppermute(near_a[: ROWS // 2], "tok", turn(1))
    far_b = lax.ppermute(near_b[ROWS // 2 :], "tok", turn(3))
    cam_ctx = call(
        "camera_attention",
        camera_kernel,
        [CAMS] * 4 + [XCOL, WCOL, WCOL],
        CTX,
        shape(D, ROWS, dtype=jnp.float32),
        [pltpu.VMEM((2 * PIECES, D), BF)],
        work=4 * 128 * D * D + 16 * ROWS * 128 * D,
    )(*cam_parts, cq, cross_key, cross_value)
    state = call_part("cross_own", [mine], [], cq, cross_key, cross_value)
    state = call_part("cross_near", [near_a, near_b], state, cq, cross_key, cross_value)
    return call_last(
        "cross_far",
        [far_a, far_b],
        [cam_ctx],
        (cq, cross_key, cross_value, cross_output),
        state,
        base,
    )


def solution(mesh):
    split = Mesh(mesh.devices.reshape(4, 2, 4, 2, 4), ("x", "zl", "zh", "core", "tok"))
    rows = P(("x", "zl", "zh", "core", "tok"), None)
    return jax.shard_map(
        local, mesh=split, in_specs=(rows,) + (P(),) * 16, out_specs=rows, check_vma=False
    )
```

```python
import functools

import jax
import jax.numpy as jnp
from jax import lax
from jax.experimental import pallas as pl
from jax.experimental.pallas import tpu as pltpu
from jax.sharding import Mesh, PartitionSpec as P

D = 768
HDIM = 64
COLS = 256
STEPS = D // COLS
HEADS = COLS // HDIM
ROUTE = ("core", "zh", "zl", "x")
ROWS = 256
PIECES = 64
VIEW = 1024
BF = jnp.bfloat16


def norm(wide, gain, shift):
    center = jnp.mean(wide, axis=-1, keepdims=True)
    spread = jnp.mean((wide - center) ** 2, axis=-1, keepdims=True)
    return ((wide - center) * lax.rsqrt(spread + 1e-06) * gain + shift).astype(BF)


def mm(left, right):
    return lax.dot_general(left, right, (((1,), (0,)), ((), ())), preferred_element_type=jnp.float32)


def mm_nt(left, right):
    return lax.dot_general(left, right, (((1,), (1,)), ((), ())), preferred_element_type=jnp.float32)


def heads(q, k, v):
    lane = lax.broadcasted_iota(jnp.int32, q.shape, 1) // HDIM
    score = lambda head: mm_nt(jnp.where(lane == head, q, jnp.zeros_like(q)), k)
    ahead = score(0)
    for head in range(HEADS):
        s = ahead
        if head + 1 < HEADS:
            ahead = score(head + 1)
        top = jnp.max(s, axis=-1, keepdims=True)
        p = jnp.exp(s - top)
        yield lane == head, top, jnp.sum(p, axis=-1, keepdims=True), mm(p.astype(BF), v)


def attend(q, k, v):
    out = None
    for mine, _, total, c in heads(q, k, v):
        c = c / total
        out = c if out is None else jnp.where(mine, c, out)
    return out


def heads_t(q, k, vt):
    lane = lax.broadcasted_iota(jnp.int32, q.shape, 1) // HDIM
    score = lambda head: mm_nt(k, jnp.where(lane == head, q, jnp.zeros_like(q)))
    ahead = score(0)
    for head in range(HEADS):
        s = ahead
        if head + 1 < HEADS:
            ahead = score(head + 1)
        top = jnp.max(s, axis=0, keepdims=True)
        p = jnp.exp(s - top)
        c = mm(vt[HDIM * head : HDIM * (head + 1)], p.astype(BF))
        yield slice(HDIM * head, HDIM * (head + 1)), head, top, jnp.sum(p, axis=0, keepdims=True), c


def mm_tn(left, right):
    return lax.dot_general(left, right, (((0,), (0,)), ((), ())), preferred_element_type=jnp.float32)


def pack_kernel(cams, x_ref, gain, shift, o_ref):
    group = lax.axis_index(("x", "zl"))
    view = lax.axis_index(("zh", "core"))
    tok = lax.axis_index("tok")
    row = cams[group, 2 * view + tok // 2] - (view * VIEW + tok * ROWS)
    m = norm(x_ref[...].astype(jnp.float32), gain[...][None], shift[...][None])
    pick = (lax.broadcasted_iota(jnp.int32, (8, ROWS), 1) == row).astype(BF)
    cam = mm(pick, m)
    sub = lax.broadcasted_iota(jnp.int32, (8, 128), 0)
    extra = jnp.zeros((8, 128), jnp.float32)
    for c in range(D // 128):
        extra = jnp.where(sub == c, cam[:, 128 * c : 128 * (c + 1)], extra)
        tiles = m[:, 128 * c : 128 * (c + 1)].astype(jnp.float32).reshape(ROWS // 8, 8, 128)
        o_ref[:, c // 3, c % 3] = tiles.astype(BF)
    spread = jnp.broadcast_to(extra[None], (ROWS // 8, 8, 128)).astype(BF)
    o_ref[:, 0, 3] = spread
    o_ref[:, 1, 3] = spread


def norm_kernel(x_ref, gain, shift, o_ref):
    o_ref[...] = norm(x_ref[...].astype(jnp.float32), gain[...][None], shift[...][None])


def query_kernel(x_ref, h_ref, gain, shift, wc, ws, c_ref, s_ref, n_ref):
    @pl.when(pl.program_id(0) == 0)
    def _():
        n_ref[...] = norm(x_ref[...].astype(jnp.float32), gain[...][None], shift[...][None])

    c_ref[...] = mm(n_ref[...], wc[...]).astype(BF) * BF(0.125)
    s_ref[...] = mm(h_ref[...], ws[...]).astype(BF) * BF(0.125)


def camera_kernel(p0, p1, p2, p3, q_ref, wk, wv, c_ref, m_ref):
    @pl.when(pl.program_id(0) == 0)
    def _():
        tok = lax.axis_index("tok")
        parts = [ref[...].astype(jnp.float32) for ref in (p0, p1, p2, p3)]
        for half in (0, 1):
            total = jnp.zeros((PIECES, 8, 128), jnp.float32)
            for shift, part in zip((0, 1, 3, 2), parts):
                total += jnp.where((tok + 4 - shift) % 4 // 2 == half, part, 0.0)
            for c in range(D // 128):
                m_ref[PIECES * half : PIECES * (half + 1), 128 * c : 128 * (c + 1)] = total[
                    :, c, :
                ].astype(BF)

    m = m_ref[...]
    k = mm(m, wk[...]).astype(BF)
    v = mm(m, wv[...]).astype(BF)
    for at, _, _, total, c in heads_t(q_ref[...], k, jnp.transpose(v)):
        c_ref[at] = c * (1.0 / total)


def keys_values(blocks, wk, wv):
    m = blocks[0][...] if len(blocks) == 1 else jnp.concatenate([r[...] for r in blocks], axis=0)
    return mm(m, wk[...]).astype(BF), jnp.transpose(mm(m, wv[...]).astype(BF))


def merged(parts, state):
    c_ref, t_ref, l_ref = state
    for at, head, top, total, c in parts:
        top0 = t_ref[head : head + 1]
        best = jnp.maximum(top, top0)
        w0 = jnp.exp(top0 - best)
        w1 = jnp.exp(top - best)
        yield at, head, best, w0 * l_ref[head : head + 1] + w1 * total, c_ref[at] * w0 + c * w1


def column_parts(step, q_ref, wk, wv, m, state):
    at = slice(step * COLS, (step + 1) * COLS)
    k = mm(m, wk[:, at]).astype(BF)
    vt = jnp.transpose(mm(m, wv[:, at]).astype(BF))
    parts = heads_t(q_ref[:, at], k, vt)
    if not state:
        return parts
    c_ref, t_ref, l_ref = state
    rows = pl.ds(step * 8, 8)
    return merged(parts, (c_ref.at[pl.ds(step * COLS, COLS)], t_ref.at[rows], l_ref.at[rows]))


def joined(blocks):
    return blocks[0][...] if len(blocks) == 1 else jnp.concatenate([r[...] for r in blocks], axis=0)


def part_kernel(blocks, *refs):
    q_ref, wk, wv, c_ref, t_ref, l_ref = refs[blocks:][-6:]
    m = joined(refs[:blocks])
    for step in range(STEPS):
        for at, head, top, total, c in column_parts(
            step, q_ref, wk, wv, m, refs[blocks : len(refs) - 6]
        ):
            c_ref[step * COLS + at.start : step * COLS + at.stop] = c
            t_ref[step * 8 + head : step * 8 + head + 1] = top
            l_ref[step * 8 + head : step * 8 + head + 1] = total


def last_kernel(blocks, *refs):
    extra, q_ref, wk, wv, wo, c_ref, t_ref, l_ref, b_ref, o_ref = refs[blocks:]
    m = joined(refs[:blocks])
    ctx = []
    for step in range(STEPS):
        for at, _, _, total, c in column_parts(step, q_ref, wk, wv, m, (c_ref, t_ref, l_ref)):
            c = c * (1.0 / total) + extra[step * COLS + at.start : step * COLS + at.stop]
            ctx.append(c.astype(BF))
    o_ref[...] = b_ref[...] + mm_tn(jnp.concatenate(ctx, axis=0), wo[...])


def others_kernel(*refs):
    h1, h2, h3, wk, q, wv, c, t, l, x, wo = refs[:11]
    o_ref = refs[11]
    hb, kb, qb, vb, cb, tb, lb, xb, ob, sems = refs[12:]
    moves = {}

    def start(name, src, dst):
        moves[name] = pltpu.make_async_copy(src, dst, sems.at[len(moves)])
        moves[name].start()

    def weights(step):
        at = pl.ds(step * COLS, COLS)
        start(("k", step), wk.at[:, at], kb.at[:, at])
        start(("v", step), wv.at[:, at], vb.at[:, at])

    for i, h in enumerate((h1, h2, h3)):
        start(("h", i), h, hb.at[pl.ds(i * ROWS, ROWS)])
        if i == 0:
            weights(0)
    start("q", q, qb)
    ctx = []
    for step in range(STEPS):
        at = slice(step * COLS, (step + 1) * COLS)
        moves[("k", step)].wait()
        moves[("v", step)].wait()
        if step == 0:
            for i in range(3):
                moves[("h", i)].wait()
            moves["q"].wait()
            for name, src, dst in (("c", c, cb), ("t", t, tb), ("l", l, lb)):
                start(name, src, dst)
        if step + 1 < STEPS:
            weights(step + 1)
        if step == 1:
            start("x", x, xb)
            start("o", wo, ob)
        k = mm(hb[...], kb[:, at]).astype(BF)
        vt = jnp.transpose(mm(hb[...], vb[:, at]).astype(BF))
        parts = heads_t(qb[:, at], k, vt)
        if step == 0:
            for name in "ctl":
                moves[name].wait()
        state = (
            cb.at[pl.ds(step * COLS, COLS)],
            tb.at[pl.ds(step * 8, 8)],
            lb.at[pl.ds(step * 8, 8)],
        )
        for _, _, _, total, value in merged(parts, state):
            ctx.append((value * (1.0 / total)).astype(BF))
    moves["x"].wait()
    moves["o"].wait()
    o_ref[...] = xb[...].astype(jnp.float32) + mm_tn(jnp.concatenate(ctx, axis=0), ob[...])


def call_others(others, q, wk, wv, wo, state, tokens):
    operands = (*others, wk, q, wv, *state, tokens, wo)
    buffers = [(3 * ROWS, D), (D, D), (ROWS, D), (D, D)]
    return pl.pallas_call(
        others_kernel,
        in_specs=[pl.BlockSpec(memory_space=pl.ANY)] * len(operands),
        out_specs=pl.BlockSpec(memory_space=pltpu.VMEM),
        out_shape=shape(ROWS, D, dtype=jnp.float32),
        scratch_shapes=[pltpu.VMEM(dims, BF) for dims in buffers]
        + [pltpu.VMEM(value.shape, value.dtype) for value in (*state, tokens, wo)]
        + [pltpu.SemaphoreType.DMA((15,))],
        compiler_params=pltpu.CompilerParams(vmem_limit_bytes=63 * 1024 * 1024),
        cost_estimate=pl.CostEstimate(
            flops=12 * ROWS * D * D + 48 * ROWS * ROWS * D,
            bytes_accessed=8 * D * D,
            transcendentals=0,
        ),
        name="self_others",
    )(*operands)


def full(shape):
    return pl.BlockSpec(shape, lambda i: (0,) * len(shape))


WCOL = pl.BlockSpec((D, COLS), lambda i: (0, i))
WROW = pl.BlockSpec((COLS, D), lambda i: (i, 0))
XCOL = pl.BlockSpec((ROWS, COLS), lambda i: (0, i))
CTX = pl.BlockSpec((COLS, ROWS), lambda i: (i, 0))
STAT = pl.BlockSpec((8, ROWS), lambda i: (i, 0))
VEC = full((D,))
X = full((ROWS, D))
W = full((D, D))
ALL = full((D, ROWS))
ALLSTAT = full((8 * STEPS, ROWS))
HALF = full((ROWS // 2, D))
CAMS = full((PIECES, 8, 128))


def shape(*dims, dtype=BF):
    return jax.ShapeDtypeStruct(dims, dtype)


def call(name, kernel, ins, outs, out_shape, scratch=(), steps=STEPS, work=0, limit=32):
    return pl.pallas_call(
        kernel,
        grid=(steps,),
        in_specs=ins,
        out_specs=outs,
        out_shape=out_shape,
        scratch_shapes=list(scratch),
        compiler_params=pltpu.CompilerParams(
            dimension_semantics=("arbitrary",), vmem_limit_bytes=limit * 1024 * 1024
        ),
        cost_estimate=pl.CostEstimate(
            flops=work, bytes_accessed=2 * D * D * 2, transcendentals=0
        ),
        name=name,
    )


def call_pack(camera_rows, tokens, gain, shift):
    vmem = pl.BlockSpec(memory_space=pltpu.VMEM)
    return pl.pallas_call(
        pack_kernel,
        in_specs=[pl.BlockSpec(memory_space=pltpu.SMEM), vmem, vmem, vmem],
        out_specs=vmem,
        out_shape=shape(ROWS // 8, 2, 4, 8, 128),
        name="memory_norm",
    )(camera_rows, tokens, gain, shift)


def call_part(name, blocks, state, *rest):
    rows = sum(b.shape[0] for b in blocks)
    return call(
        name,
        functools.partial(part_kernel, len(blocks)),
        [full(b.shape) for b in blocks] + [ALL, ALLSTAT, ALLSTAT][: len(state)] + [X, W, W],
        [ALL, ALLSTAT, ALLSTAT],
        [shape(n, ROWS, dtype=jnp.float32) for n in (D, 8 * STEPS, 8 * STEPS)],
        steps=1,
        work=4 * rows * D * D + 16 * rows * ROWS * D,
    )(*blocks, *state, *rest)


def call_last(name, blocks, extra, rest, state, base, limit=32):
    rows = sum(b.shape[0] for b in blocks)
    return call(
        name,
        functools.partial(last_kernel, len(blocks)),
        [full(b.shape) for b in blocks]
        + [ALL] * len(extra)
        + [X, W, W, W, ALL, ALLSTAT, ALLSTAT, X],
        X,
        shape(ROWS, D, dtype=jnp.float32),
        steps=1,
        work=4 * rows * D * D + 16 * rows * ROWS * D + 2 * ROWS * D * D,
        limit=limit,
    )(*blocks, *extra, *rest, *state, base)


def to_tiles(x):
    return x.reshape(32, 8, 6, 128).transpose(0, 2, 1, 3).reshape(PIECES, 24, 128)


def from_tiles(pieces):
    return pieces.reshape(32, 6, 8, 128).transpose(0, 2, 1, 3).reshape(ROWS, D)


def turn(shift):
    return [(i, (i + shift) % 4) for i in range(4)]


def around(value):
    return [lax.ppermute(value, "tok", turn(shift)) for shift in (1, 3, 2)]


def local(
    tokens,
    self_gain,
    self_shift,
    query_gain,
    query_shift,
    memory_gain,
    memory_shift,
    self_query,
    self_key,
    self_value,
    self_output,
    cross_query,
    cross_key,
    cross_value,
    cross_output,
    partner,
    camera_rows,
):
    packed = call_pack(camera_rows, tokens, memory_gain, memory_shift).reshape(PIECES, 32, 128)
    first = lax.all_to_all(packed, ROUTE, split_axis=0, concat_axis=0, tiled=True)
    wanted = partner.reshape(4, 2, 4, 2).transpose(3, 2, 1, 0).reshape(PIECES)
    place = (wanted % 2) * 32 + (wanted // 2 % 4) * 8 + (wanted // 8 % 2) * 4 + wanted // 16
    place = (place[:, None] * 4 + jnp.arange(3)[None, :]).reshape(PIECES * 3)
    onward = first.reshape(PIECES * 4, 8, 128).at[place].get(mode="promise_in_bounds")
    onward = onward.reshape(PIECES, 24, 128)
    cam_own = first[:, 24:]

    hidden = call("self_norm", norm_kernel, [X, VEC, VEC], X, shape(ROWS, D), steps=1)(
        tokens, self_gain, self_shift
    )
    others = around(hidden)
    cq, sq = call(
        "queries",
        query_kernel,
        [X, X, VEC, VEC, WCOL, WCOL],
        [XCOL, XCOL],
        [shape(ROWS, D), shape(ROWS, D)],
        [pltpu.VMEM((ROWS, D), BF)],
        work=4 * ROWS * D * D,
    )(tokens, hidden, query_gain, query_shift, cross_query, self_query)
    self_state = call_part("self_own", [hidden], [], sq, self_key, self_value)
    *self_state, onward = lax.optimization_barrier((*self_state, onward))
    base = call_others(
        others, sq, self_key, self_value, self_output, self_state, tokens
    )

    mine = lax.all_to_all(onward, ROUTE, split_axis=0, concat_axis=0, tiled=True)
    cam_parts = [cam_own] + around(cam_own)
    mine, base, *cam_parts[1:] = lax.optimization_barrier((mine, base, *cam_parts[1:]))
    mine = from_tiles(mine)
    near_a = lax.ppermute(mine, "tok", turn(1))
    near_b = lax.ppermute(mine, "tok", turn(3))
    far_a = lax.ppermute(near_a[: ROWS // 2], "tok", turn(1))
    far_b = lax.ppermute(near_b[ROWS // 2 :], "tok", turn(3))
    cam_ctx = call(
        "camera_attention",
        camera_kernel,
        [CAMS] * 4 + [XCOL, WCOL, WCOL],
        CTX,
        shape(D, ROWS, dtype=jnp.float32),
        [pltpu.VMEM((2 * PIECES, D), BF)],
        work=4 * 128 * D * D + 16 * ROWS * 128 * D,
    )(*cam_parts, cq, cross_key, cross_value)
    state = call_part("cross_own", [mine], [], cq, cross_key, cross_value)
    state = call_part("cross_near", [near_a, near_b], state, cq, cross_key, cross_value)
    return call_last(
        "cross_far",
        [far_a, far_b],
        [cam_ctx],
        (cq, cross_key, cross_value, cross_output),
        state,
        base,
    )


def solution(mesh):
    split = Mesh(mesh.devices.reshape(4, 2, 4, 2, 4), ("x", "zl", "zh", "core", "tok"))
    rows = P(("x", "zl", "zh", "core", "tok"), None)
    return jax.shard_map(
        local, mesh=split, in_specs=(rows,) + (P(),) * 16, out_specs=rows, check_vma=False
    )
```

```python
import functools

import jax
import jax.numpy as jnp
from jax import lax
from jax.experimental import pallas as pl
from jax.experimental.pallas import tpu as pltpu
from jax.sharding import Mesh, PartitionSpec as P

D = 768
HDIM = 64
COLS = 256
STEPS = D // COLS
HEADS = COLS // HDIM
ROUTE = ("core", "zh", "zl", "x")
ROWS = 256
PIECES = 64
VIEW = 1024
BF = jnp.bfloat16


def norm(wide, gain, shift):
    center = jnp.mean(wide, axis=-1, keepdims=True)
    spread = jnp.mean((wide - center) ** 2, axis=-1, keepdims=True)
    return ((wide - center) * lax.rsqrt(spread + 1e-06) * gain + shift).astype(BF)


def mm(left, right):
    return lax.dot_general(left, right, (((1,), (0,)), ((), ())), preferred_element_type=jnp.float32)


def mm_nt(left, right):
    return lax.dot_general(left, right, (((1,), (1,)), ((), ())), preferred_element_type=jnp.float32)


def heads(q, k, v):
    lane = lax.broadcasted_iota(jnp.int32, q.shape, 1) // HDIM
    score = lambda head: mm_nt(jnp.where(lane == head, q, jnp.zeros_like(q)), k)
    ahead = score(0)
    for head in range(HEADS):
        s = ahead
        if head + 1 < HEADS:
            ahead = score(head + 1)
        top = jnp.max(s, axis=-1, keepdims=True)
        p = jnp.exp(s - top)
        yield lane == head, top, jnp.sum(p, axis=-1, keepdims=True), mm(p.astype(BF), v)


def attend(q, k, v):
    out = None
    for mine, _, total, c in heads(q, k, v):
        c = c / total
        out = c if out is None else jnp.where(mine, c, out)
    return out


def heads_t(q, k, vt):
    lane = lax.broadcasted_iota(jnp.int32, q.shape, 1) // HDIM
    score = lambda head: mm_nt(k, jnp.where(lane == head, q, jnp.zeros_like(q)))
    ahead = score(0)
    for head in range(HEADS):
        s = ahead
        if head + 1 < HEADS:
            ahead = score(head + 1)
        top = jnp.max(s, axis=0, keepdims=True)
        p = jnp.exp(s - top)
        c = mm(vt[HDIM * head : HDIM * (head + 1)], p.astype(BF))
        yield slice(HDIM * head, HDIM * (head + 1)), head, top, jnp.sum(p, axis=0, keepdims=True), c


def mm_tn(left, right):
    return lax.dot_general(left, right, (((0,), (0,)), ((), ())), preferred_element_type=jnp.float32)


def pack_kernel(cams, x_ref, gain, shift, o_ref):
    group = lax.axis_index(("x", "zl"))
    view = lax.axis_index(("zh", "core"))
    tok = lax.axis_index("tok")
    row = cams[group, 2 * view + tok // 2] - (view * VIEW + tok * ROWS)
    m = norm(x_ref[...].astype(jnp.float32), gain[...][None], shift[...][None])
    pick = (lax.broadcasted_iota(jnp.int32, (8, ROWS), 1) == row).astype(BF)
    cam = mm(pick, m)
    sub = lax.broadcasted_iota(jnp.int32, (8, 128), 0)
    extra = jnp.zeros((8, 128), jnp.float32)
    for c in range(D // 128):
        extra = jnp.where(sub == c, cam[:, 128 * c : 128 * (c + 1)], extra)
        tiles = m[:, 128 * c : 128 * (c + 1)].astype(jnp.float32).reshape(ROWS // 8, 8, 128)
        o_ref[:, c // 3, c % 3] = tiles.astype(BF)
    spread = jnp.broadcast_to(extra[None], (ROWS // 8, 8, 128)).astype(BF)
    o_ref[:, 0, 3] = spread
    o_ref[:, 1, 3] = spread


def norm_kernel(x_ref, gain, shift, o_ref):
    o_ref[...] = norm(x_ref[...].astype(jnp.float32), gain[...][None], shift[...][None])


def query_kernel(x_ref, h_ref, gain, shift, wc, ws, c_ref, s_ref, n_ref):
    @pl.when(pl.program_id(0) == 0)
    def _():
        n_ref[...] = norm(x_ref[...].astype(jnp.float32), gain[...][None], shift[...][None])

    c_ref[...] = mm(n_ref[...], wc[...]).astype(BF) * BF(0.125)
    s_ref[...] = mm(h_ref[...], ws[...]).astype(BF) * BF(0.125)


def camera_kernel(p0, p1, p2, p3, q_ref, wk, wv, c_ref):
    tok = lax.axis_index("tok")
    parts = [ref[...].astype(jnp.float32) for ref in (p0, p1, p2, p3)]
    first = [(tok + 4 - shift) % 4 // 2 == 0 for shift in (0, 1, 3, 2)]
    halves = []
    for want in (True, False):
        total = jnp.zeros((PIECES, 8, 128), jnp.float32)
        for flag, part in zip(first, parts):
            total += jnp.where(flag == want, part, 0.0)
        halves.append(jnp.concatenate([total[:, c, :] for c in range(D // 128)], axis=1))
    m = jnp.concatenate(halves, axis=0).astype(BF)
    for step in range(STEPS):
        for at, _, _, total, c in column_parts(step, q_ref, wk, wv, m, ()):
            c_ref[step * COLS + at.start : step * COLS + at.stop] = c * (1.0 / total)


def keys_values(blocks, wk, wv):
    m = blocks[0][...] if len(blocks) == 1 else jnp.concatenate([r[...] for r in blocks], axis=0)
    return mm(m, wk[...]).astype(BF), jnp.transpose(mm(m, wv[...]).astype(BF))


def merged(parts, state):
    c_ref, t_ref, l_ref = state
    for at, head, top, total, c in parts:
        top0 = t_ref[head : head + 1]
        best = jnp.maximum(top, top0)
        w0 = jnp.exp(top0 - best)
        w1 = jnp.exp(top - best)
        yield at, head, best, w0 * l_ref[head : head + 1] + w1 * total, c_ref[at] * w0 + c * w1


def column_parts(step, q_ref, wk, wv, m, state):
    at = slice(step * COLS, (step + 1) * COLS)
    k = mm(m, wk[:, at]).astype(BF)
    vt = jnp.transpose(mm(m, wv[:, at]).astype(BF))
    parts = heads_t(q_ref[:, at], k, vt)
    if not state:
        return parts
    c_ref, t_ref, l_ref = state
    rows = pl.ds(step * 8, 8)
    return merged(parts, (c_ref.at[pl.ds(step * COLS, COLS)], t_ref.at[rows], l_ref.at[rows]))


def joined(blocks):
    return blocks[0][...] if len(blocks) == 1 else jnp.concatenate([r[...] for r in blocks], axis=0)


def part_kernel(blocks, *refs):
    q_ref, wk, wv, c_ref, t_ref, l_ref = refs[blocks:][-6:]
    m = joined(refs[:blocks])
    for step in range(STEPS):
        for at, head, top, total, c in column_parts(
            step, q_ref, wk, wv, m, refs[blocks : len(refs) - 6]
        ):
            c_ref[step * COLS + at.start : step * COLS + at.stop] = c
            t_ref[step * 8 + head : step * 8 + head + 1] = top
            l_ref[step * 8 + head : step * 8 + head + 1] = total


def last_kernel(blocks, *refs):
    extra, q_ref, wk, wv, wo, c_ref, t_ref, l_ref, b_ref, o_ref = refs[blocks:]
    m = joined(refs[:blocks])
    ctx = []
    for step in range(STEPS):
        for at, _, _, total, c in column_parts(step, q_ref, wk, wv, m, (c_ref, t_ref, l_ref)):
            c = c * (1.0 / total) + extra[step * COLS + at.start : step * COLS + at.stop]
            ctx.append(c.astype(BF))
    o_ref[...] = b_ref[...] + mm_tn(jnp.concatenate(ctx, axis=0), wo[...])


def others_kernel(*refs):
    h1, h2, h3, wk, q, wv, c, t, l, x, wo = refs[:11]
    o_ref = refs[11]
    hb, kb, qb, vb, cb, tb, lb, xb, ob, sems = refs[12:]
    moves = {}

    def start(name, src, dst):
        moves[name] = pltpu.make_async_copy(src, dst, sems.at[len(moves)])
        moves[name].start()

    def weights(step):
        at = pl.ds(step * COLS, COLS)
        start(("k", step), wk.at[:, at], kb.at[:, at])
        start(("v", step), wv.at[:, at], vb.at[:, at])

    for i, h in enumerate((h1, h2, h3)):
        start(("h", i), h, hb.at[pl.ds(i * ROWS, ROWS)])
        if i == 0:
            weights(0)
    start("q", q, qb)
    ctx = []
    for step in range(STEPS):
        at = slice(step * COLS, (step + 1) * COLS)
        moves[("k", step)].wait()
        moves[("v", step)].wait()
        if step == 0:
            for i in range(3):
                moves[("h", i)].wait()
            moves["q"].wait()
            for name, src, dst in (("c", c, cb), ("t", t, tb), ("l", l, lb)):
                start(name, src, dst)
        if step + 1 < STEPS:
            weights(step + 1)
        if step == 1:
            start("x", x, xb)
            start("o", wo, ob)
        k = mm(hb[...], kb[:, at]).astype(BF)
        vt = jnp.transpose(mm(hb[...], vb[:, at]).astype(BF))
        parts = heads_t(qb[:, at], k, vt)
        if step == 0:
            for name in "ctl":
                moves[name].wait()
        state = (
            cb.at[pl.ds(step * COLS, COLS)],
            tb.at[pl.ds(step * 8, 8)],
            lb.at[pl.ds(step * 8, 8)],
        )
        for _, _, _, total, value in merged(parts, state):
            ctx.append((value * (1.0 / total)).astype(BF))
    moves["x"].wait()
    moves["o"].wait()
    o_ref[...] = xb[...].astype(jnp.float32) + mm_tn(jnp.concatenate(ctx, axis=0), ob[...])


def call_others(others, q, wk, wv, wo, state, tokens):
    operands = (*others, wk, q, wv, *state, tokens, wo)
    buffers = [(3 * ROWS, D), (D, D), (ROWS, D), (D, D)]
    return pl.pallas_call(
        others_kernel,
        in_specs=[pl.BlockSpec(memory_space=pl.ANY)] * len(operands),
        out_specs=pl.BlockSpec(memory_space=pltpu.VMEM),
        out_shape=shape(ROWS, D, dtype=jnp.float32),
        scratch_shapes=[pltpu.VMEM(dims, BF) for dims in buffers]
        + [pltpu.VMEM(value.shape, value.dtype) for value in (*state, tokens, wo)]
        + [pltpu.SemaphoreType.DMA((15,))],
        compiler_params=pltpu.CompilerParams(vmem_limit_bytes=63 * 1024 * 1024),
        cost_estimate=pl.CostEstimate(
            flops=12 * ROWS * D * D + 48 * ROWS * ROWS * D,
            bytes_accessed=8 * D * D,
            transcendentals=0,
        ),
        name="self_others",
    )(*operands)


def full(shape):
    return pl.BlockSpec(shape, lambda i: (0,) * len(shape))


WCOL = pl.BlockSpec((D, COLS), lambda i: (0, i))
WROW = pl.BlockSpec((COLS, D), lambda i: (i, 0))
XCOL = pl.BlockSpec((ROWS, COLS), lambda i: (0, i))
CTX = pl.BlockSpec((COLS, ROWS), lambda i: (i, 0))
STAT = pl.BlockSpec((8, ROWS), lambda i: (i, 0))
VEC = full((D,))
X = full((ROWS, D))
W = full((D, D))
ALL = full((D, ROWS))
ALLSTAT = full((8 * STEPS, ROWS))
HALF = full((ROWS // 2, D))
CAMS = full((PIECES, 8, 128))


def shape(*dims, dtype=BF):
    return jax.ShapeDtypeStruct(dims, dtype)


def call(name, kernel, ins, outs, out_shape, scratch=(), steps=STEPS, work=0, limit=32):
    return pl.pallas_call(
        kernel,
        grid=(steps,),
        in_specs=ins,
        out_specs=outs,
        out_shape=out_shape,
        scratch_shapes=list(scratch),
        compiler_params=pltpu.CompilerParams(
            dimension_semantics=("arbitrary",), vmem_limit_bytes=limit * 1024 * 1024
        ),
        cost_estimate=pl.CostEstimate(
            flops=work, bytes_accessed=2 * D * D * 2, transcendentals=0
        ),
        name=name,
    )


def call_pack(camera_rows, tokens, gain, shift):
    vmem = pl.BlockSpec(memory_space=pltpu.VMEM)
    return pl.pallas_call(
        pack_kernel,
        in_specs=[pl.BlockSpec(memory_space=pltpu.SMEM), vmem, vmem, vmem],
        out_specs=vmem,
        out_shape=shape(ROWS // 8, 2, 4, 8, 128),
        name="memory_norm",
    )(camera_rows, tokens, gain, shift)


def call_part(name, blocks, state, *rest):
    rows = sum(b.shape[0] for b in blocks)
    return call(
        name,
        functools.partial(part_kernel, len(blocks)),
        [full(b.shape) for b in blocks] + [ALL, ALLSTAT, ALLSTAT][: len(state)] + [X, W, W],
        [ALL, ALLSTAT, ALLSTAT],
        [shape(n, ROWS, dtype=jnp.float32) for n in (D, 8 * STEPS, 8 * STEPS)],
        steps=1,
        work=4 * rows * D * D + 16 * rows * ROWS * D,
    )(*blocks, *state, *rest)


def call_last(name, blocks, extra, rest, state, base, limit=32):
    rows = sum(b.shape[0] for b in blocks)
    return call(
        name,
        functools.partial(last_kernel, len(blocks)),
        [full(b.shape) for b in blocks]
        + [ALL] * len(extra)
        + [X, W, W, W, ALL, ALLSTAT, ALLSTAT, X],
        X,
        shape(ROWS, D, dtype=jnp.float32),
        steps=1,
        work=4 * rows * D * D + 16 * rows * ROWS * D + 2 * ROWS * D * D,
        limit=limit,
    )(*blocks, *extra, *rest, *state, base)


def to_tiles(x):
    return x.reshape(32, 8, 6, 128).transpose(0, 2, 1, 3).reshape(PIECES, 24, 128)


def from_tiles(pieces):
    return pieces.reshape(32, 6, 8, 128).transpose(0, 2, 1, 3).reshape(ROWS, D)


def turn(shift):
    return [(i, (i + shift) % 4) for i in range(4)]


def around(value):
    return [lax.ppermute(value, "tok", turn(shift)) for shift in (1, 3, 2)]


def local(
    tokens,
    self_gain,
    self_shift,
    query_gain,
    query_shift,
    memory_gain,
    memory_shift,
    self_query,
    self_key,
    self_value,
    self_output,
    cross_query,
    cross_key,
    cross_value,
    cross_output,
    partner,
    camera_rows,
):
    packed = call_pack(camera_rows, tokens, memory_gain, memory_shift).reshape(PIECES, 32, 128)
    first = lax.all_to_all(packed, ROUTE, split_axis=0, concat_axis=0, tiled=True)
    wanted = partner.reshape(4, 2, 4, 2).transpose(3, 2, 1, 0).reshape(PIECES)
    place = (wanted % 2) * 32 + (wanted // 2 % 4) * 8 + (wanted // 8 % 2) * 4 + wanted // 16
    place = (place[:, None] * 4 + jnp.arange(3)[None, :]).reshape(PIECES * 3)
    onward = first.reshape(PIECES * 4, 8, 128).at[place].get(mode="promise_in_bounds")
    onward = onward.reshape(PIECES, 24, 128)
    cam_own = first[:, 24:]

    hidden = call("self_norm", norm_kernel, [X, VEC, VEC], X, shape(ROWS, D), steps=1)(
        tokens, self_gain, self_shift
    )
    others = around(hidden)
    cq, sq = call(
        "queries",
        query_kernel,
        [X, X, VEC, VEC, WCOL, WCOL],
        [XCOL, XCOL],
        [shape(ROWS, D), shape(ROWS, D)],
        [pltpu.VMEM((ROWS, D), BF)],
        work=4 * ROWS * D * D,
    )(tokens, hidden, query_gain, query_shift, cross_query, self_query)
    self_state = call_part("self_own", [hidden], [], sq, self_key, self_value)
    *self_state, onward = lax.optimization_barrier((*self_state, onward))
    base = call_others(
        others, sq, self_key, self_value, self_output, self_state, tokens
    )

    mine = lax.all_to_all(onward, ROUTE, split_axis=0, concat_axis=0, tiled=True)
    cam_parts = [cam_own] + around(cam_own)
    mine, base, *cam_parts[1:] = lax.optimization_barrier((mine, base, *cam_parts[1:]))
    mine = from_tiles(mine)
    near_a = lax.ppermute(mine, "tok", turn(1))
    near_b = lax.ppermute(mine, "tok", turn(3))
    far_a = lax.ppermute(near_a[: ROWS // 2], "tok", turn(1))
    far_b = lax.ppermute(near_b[ROWS // 2 :], "tok", turn(3))
    cam_ctx = call(
        "camera_attention",
        camera_kernel,
        [CAMS] * 4 + [X, W, W],
        ALL,
        shape(D, ROWS, dtype=jnp.float32),
        steps=1,
        work=4 * 128 * D * D + 16 * ROWS * 128 * D,
    )(*cam_parts, cq, cross_key, cross_value)
    state = call_part("cross_own", [mine], [], cq, cross_key, cross_value)
    state = call_part("cross_near", [near_a, near_b], state, cq, cross_key, cross_value)
    return call_last(
        "cross_far",
        [far_a, far_b],
        [cam_ctx],
        (cq, cross_key, cross_value, cross_output),
        state,
        base,
    )


def solution(mesh):
    split = Mesh(mesh.devices.reshape(4, 2, 4, 2, 4), ("x", "zl", "zh", "core", "tok"))
    rows = P(("x", "zl", "zh", "core", "tok"), None)
    return jax.shard_map(
        local, mesh=split, in_specs=(rows,) + (P(),) * 16, out_specs=rows, check_vma=False
    )
```

```python
import functools

import jax
import jax.numpy as jnp
from jax import lax
from jax.experimental import pallas as pl
from jax.experimental.pallas import tpu as pltpu
from jax.sharding import Mesh, PartitionSpec as P

D = 768
HDIM = 64
COLS = 256
STEPS = D // COLS
HEADS = COLS // HDIM
ROUTE = ("core", "zh", "zl", "x")
ROWS = 256
PIECES = 64
VIEW = 1024
BF = jnp.bfloat16


def norm(wide, gain, shift):
    center = jnp.mean(wide, axis=-1, keepdims=True)
    spread = jnp.mean((wide - center) ** 2, axis=-1, keepdims=True)
    return ((wide - center) * lax.rsqrt(spread + 1e-06) * gain + shift).astype(BF)


def mm(left, right):
    return lax.dot_general(left, right, (((1,), (0,)), ((), ())), preferred_element_type=jnp.float32)


def mm_nt(left, right):
    return lax.dot_general(left, right, (((1,), (1,)), ((), ())), preferred_element_type=jnp.float32)


def heads_stacked(q, k, vt):
    rows = q.shape[0]
    lane = lax.broadcasted_iota(jnp.int32, q.shape, 1) // HDIM
    stack = [jnp.where(lane == head, q, jnp.zeros_like(q)) for head in range(HEADS)]
    s = mm_nt(k, jnp.concatenate(stack, axis=0))
    top = jnp.max(s, axis=0, keepdims=True)
    p = jnp.exp(s - top)
    total = jnp.sum(p, axis=0, keepdims=True)
    p = p.astype(BF)
    for head in range(HEADS):
        at = slice(HDIM * head, HDIM * (head + 1))
        cols = slice(rows * head, rows * (head + 1))
        yield at, head, top[:, cols], total[:, cols], mm(vt[at], p[:, cols])


def mm_tn(left, right):
    return lax.dot_general(left, right, (((0,), (0,)), ((), ())), preferred_element_type=jnp.float32)


def pack_kernel(cams, x_ref, gain, shift, o_ref):
    group = lax.axis_index(("x", "zl"))
    view = lax.axis_index(("zh", "core"))
    tok = lax.axis_index("tok")
    row = cams[group, 2 * view + tok // 2] - (view * VIEW + tok * ROWS)
    m = norm(x_ref[...].astype(jnp.float32), gain[...][None], shift[...][None])
    pick = (lax.broadcasted_iota(jnp.int32, (8, ROWS), 1) == row).astype(BF)
    cam = mm(pick, m)
    sub = lax.broadcasted_iota(jnp.int32, (8, 128), 0)
    extra = jnp.zeros((8, 128), jnp.float32)
    for c in range(D // 128):
        extra = jnp.where(sub == c, cam[:, 128 * c : 128 * (c + 1)], extra)
        tiles = m[:, 128 * c : 128 * (c + 1)].astype(jnp.float32).reshape(ROWS // 8, 8, 128)
        o_ref[:, c // 3, c % 3] = tiles.astype(BF)
    spread = jnp.broadcast_to(extra[None], (ROWS // 8, 8, 128)).astype(BF)
    o_ref[:, 0, 3] = spread
    o_ref[:, 1, 3] = spread


def norm_kernel(x_ref, gain, shift, o_ref):
    o_ref[...] = norm(x_ref[...].astype(jnp.float32), gain[...][None], shift[...][None])


def query_kernel(x_ref, h_ref, gain, shift, wc, ws, c_ref, s_ref, n_ref):
    @pl.when(pl.program_id(0) == 0)
    def _():
        n_ref[...] = norm(x_ref[...].astype(jnp.float32), gain[...][None], shift[...][None])

    c_ref[...] = mm(n_ref[...], wc[...]).astype(BF) * BF(0.125)
    s_ref[...] = mm(h_ref[...], ws[...]).astype(BF) * BF(0.125)


def camera_kernel(p0, p1, p2, p3, q_ref, wk, wv, c_ref):
    tok = lax.axis_index("tok")
    parts = [ref[...].astype(jnp.float32) for ref in (p0, p1, p2, p3)]
    first = [(tok + 4 - shift) % 4 // 2 == 0 for shift in (0, 1, 3, 2)]
    halves = []
    for want in (True, False):
        total = jnp.zeros((PIECES, 8, 128), jnp.float32)
        for flag, part in zip(first, parts):
            total += jnp.where(flag == want, part, 0.0)
        halves.append(jnp.concatenate([total[:, c, :] for c in range(D // 128)], axis=1))
    m = jnp.concatenate(halves, axis=0).astype(BF)
    for step in range(STEPS):
        for at, _, _, total, c in column_parts(step, q_ref, wk, wv, m, ()):
            c_ref[step * COLS + at.start : step * COLS + at.stop] = c * (1.0 / total)


def merged(parts, state):
    c_ref, t_ref, l_ref = state
    for at, head, top, total, c in parts:
        top0 = t_ref[head : head + 1]
        best = jnp.maximum(top, top0)
        w0 = jnp.exp(top0 - best)
        w1 = jnp.exp(top - best)
        yield at, head, best, w0 * l_ref[head : head + 1] + w1 * total, c_ref[at] * w0 + c * w1


def column_parts(step, q_ref, wk, wv, m, state):
    at = slice(step * COLS, (step + 1) * COLS)
    k = mm(m, wk[:, at]).astype(BF)
    vt = jnp.transpose(mm(m, wv[:, at]).astype(BF))
    parts = heads_stacked(q_ref[:, at], k, vt)
    if not state:
        return parts
    c_ref, t_ref, l_ref = state
    rows = pl.ds(step * 8, 8)
    return merged(parts, (c_ref.at[pl.ds(step * COLS, COLS)], t_ref.at[rows], l_ref.at[rows]))


def joined(blocks):
    return blocks[0][...] if len(blocks) == 1 else jnp.concatenate([r[...] for r in blocks], axis=0)


def part_kernel(blocks, *refs):
    q_ref, wk, wv, c_ref, t_ref, l_ref = refs[blocks:][-6:]
    m = joined(refs[:blocks])
    for step in range(STEPS):
        for at, head, top, total, c in column_parts(
            step, q_ref, wk, wv, m, refs[blocks : len(refs) - 6]
        ):
            c_ref[step * COLS + at.start : step * COLS + at.stop] = c
            t_ref[step * 8 + head : step * 8 + head + 1] = top
            l_ref[step * 8 + head : step * 8 + head + 1] = total


def last_kernel(blocks, *refs):
    extra, q_ref, wk, wv, wo, c_ref, t_ref, l_ref, b_ref, o_ref = refs[blocks:]
    m = joined(refs[:blocks])
    ctx = []
    for step in range(STEPS):
        for at, _, _, total, c in column_parts(step, q_ref, wk, wv, m, (c_ref, t_ref, l_ref)):
            c = c * (1.0 / total) + extra[step * COLS + at.start : step * COLS + at.stop]
            ctx.append(c.astype(BF))
    o_ref[...] = b_ref[...] + mm_tn(jnp.concatenate(ctx, axis=0), wo[...])


def others_kernel(*refs):
    h1, h2, h3, wk, q, wv, c, t, l, x, wo = refs[:11]
    o_ref = refs[11]
    hb, kb, qb, vb, cb, tb, lb, xb, ob, sems = refs[12:]
    moves = {}

    def start(name, src, dst):
        moves[name] = pltpu.make_async_copy(src, dst, sems.at[len(moves)])
        moves[name].start()

    def weights(step):
        at = pl.ds(step * COLS, COLS)
        start(("k", step), wk.at[:, at], kb.at[:, at])
        start(("v", step), wv.at[:, at], vb.at[:, at])

    for i, h in enumerate((h1, h2, h3)):
        start(("h", i), h, hb.at[pl.ds(i * ROWS, ROWS)])
        if i == 0:
            weights(0)
    start("q", q, qb)
    ctx = []
    for step in range(STEPS):
        at = slice(step * COLS, (step + 1) * COLS)
        moves[("k", step)].wait()
        moves[("v", step)].wait()
        if step == 0:
            for i in range(3):
                moves[("h", i)].wait()
            moves["q"].wait()
            for name, src, dst in (("c", c, cb), ("t", t, tb), ("l", l, lb)):
                start(name, src, dst)
        if step + 1 < STEPS:
            weights(step + 1)
        if step == 1:
            start("x", x, xb)
            start("o", wo, ob)
        k = mm(hb[...], kb[:, at]).astype(BF)
        vt = jnp.transpose(mm(hb[...], vb[:, at]).astype(BF))
        parts = heads_stacked(qb[:, at], k, vt)
        if step == 0:
            for name in "ctl":
                moves[name].wait()
        state = (
            cb.at[pl.ds(step * COLS, COLS)],
            tb.at[pl.ds(step * 8, 8)],
            lb.at[pl.ds(step * 8, 8)],
        )
        for _, _, _, total, value in merged(parts, state):
            ctx.append((value * (1.0 / total)).astype(BF))
    moves["x"].wait()
    moves["o"].wait()
    o_ref[...] = xb[...].astype(jnp.float32) + mm_tn(jnp.concatenate(ctx, axis=0), ob[...])


def call_others(others, q, wk, wv, wo, state, tokens):
    operands = (*others, wk, q, wv, *state, tokens, wo)
    buffers = [(3 * ROWS, D), (D, D), (ROWS, D), (D, D)]
    return pl.pallas_call(
        others_kernel,
        in_specs=[pl.BlockSpec(memory_space=pl.ANY)] * len(operands),
        out_specs=pl.BlockSpec(memory_space=pltpu.VMEM),
        out_shape=shape(ROWS, D, dtype=jnp.float32),
        scratch_shapes=[pltpu.VMEM(dims, BF) for dims in buffers]
        + [pltpu.VMEM(value.shape, value.dtype) for value in (*state, tokens, wo)]
        + [pltpu.SemaphoreType.DMA((15,))],
        compiler_params=pltpu.CompilerParams(vmem_limit_bytes=63 * 1024 * 1024),
        cost_estimate=pl.CostEstimate(
            flops=12 * ROWS * D * D + 48 * ROWS * ROWS * D,
            bytes_accessed=8 * D * D,
            transcendentals=0,
        ),
        name="self_others",
    )(*operands)


def full(shape):
    return pl.BlockSpec(shape, lambda i: (0,) * len(shape))


WCOL = pl.BlockSpec((D, COLS), lambda i: (0, i))
XCOL = pl.BlockSpec((ROWS, COLS), lambda i: (0, i))
VEC = full((D,))
X = full((ROWS, D))
W = full((D, D))
ALL = full((D, ROWS))
ALLSTAT = full((8 * STEPS, ROWS))
HALF = full((ROWS // 2, D))
CAMS = full((PIECES, 8, 128))


def shape(*dims, dtype=BF):
    return jax.ShapeDtypeStruct(dims, dtype)


def call(name, kernel, ins, outs, out_shape, scratch=(), steps=STEPS, work=0, limit=32):
    return pl.pallas_call(
        kernel,
        grid=(steps,),
        in_specs=ins,
        out_specs=outs,
        out_shape=out_shape,
        scratch_shapes=list(scratch),
        compiler_params=pltpu.CompilerParams(
            dimension_semantics=("arbitrary",), vmem_limit_bytes=limit * 1024 * 1024
        ),
        cost_estimate=pl.CostEstimate(
            flops=work, bytes_accessed=2 * D * D * 2, transcendentals=0
        ),
        name=name,
    )


def call_pack(camera_rows, tokens, gain, shift):
    vmem = pl.BlockSpec(memory_space=pltpu.VMEM)
    return pl.pallas_call(
        pack_kernel,
        in_specs=[pl.BlockSpec(memory_space=pltpu.SMEM), vmem, vmem, vmem],
        out_specs=vmem,
        out_shape=shape(ROWS // 8, 2, 4, 8, 128),
        name="memory_norm",
    )(camera_rows, tokens, gain, shift)


def call_part(name, blocks, state, *rest):
    rows = sum(b.shape[0] for b in blocks)
    return call(
        name,
        functools.partial(part_kernel, len(blocks)),
        [full(b.shape) for b in blocks] + [ALL, ALLSTAT, ALLSTAT][: len(state)] + [X, W, W],
        [ALL, ALLSTAT, ALLSTAT],
        [shape(n, ROWS, dtype=jnp.float32) for n in (D, 8 * STEPS, 8 * STEPS)],
        steps=1,
        work=4 * rows * D * D + 16 * rows * ROWS * D,
    )(*blocks, *state, *rest)


def call_last(name, blocks, extra, rest, state, base, limit=32):
    rows = sum(b.shape[0] for b in blocks)
    return call(
        name,
        functools.partial(last_kernel, len(blocks)),
        [full(b.shape) for b in blocks]
        + [ALL] * len(extra)
        + [X, W, W, W, ALL, ALLSTAT, ALLSTAT, X],
        X,
        shape(ROWS, D, dtype=jnp.float32),
        steps=1,
        work=4 * rows * D * D + 16 * rows * ROWS * D + 2 * ROWS * D * D,
        limit=limit,
    )(*blocks, *extra, *rest, *state, base)


def to_tiles(x):
    return x.reshape(32, 8, 6, 128).transpose(0, 2, 1, 3).reshape(PIECES, 24, 128)


def from_tiles(pieces):
    return pieces.reshape(32, 6, 8, 128).transpose(0, 2, 1, 3).reshape(ROWS, D)


def turn(shift):
    return [(i, (i + shift) % 4) for i in range(4)]


def around(value):
    return [lax.ppermute(value, "tok", turn(shift)) for shift in (1, 3, 2)]


def local(
    tokens,
    self_gain,
    self_shift,
    query_gain,
    query_shift,
    memory_gain,
    memory_shift,
    self_query,
    self_key,
    self_value,
    self_output,
    cross_query,
    cross_key,
    cross_value,
    cross_output,
    partner,
    camera_rows,
):
    packed = call_pack(camera_rows, tokens, memory_gain, memory_shift).reshape(PIECES, 32, 128)
    first = lax.all_to_all(packed, ROUTE, split_axis=0, concat_axis=0, tiled=True)
    wanted = partner.reshape(4, 2, 4, 2).transpose(3, 2, 1, 0).reshape(PIECES)
    place = (wanted % 2) * 32 + (wanted // 2 % 4) * 8 + (wanted // 8 % 2) * 4 + wanted // 16
    place = (place[:, None] * 4 + jnp.arange(3)[None, :]).reshape(PIECES * 3)
    onward = first.reshape(PIECES * 4, 8, 128).at[place].get(mode="promise_in_bounds")
    onward = onward.reshape(PIECES, 24, 128)
    cam_own = first[:, 24:]

    hidden = call("self_norm", norm_kernel, [X, VEC, VEC], X, shape(ROWS, D), steps=1)(
        tokens, self_gain, self_shift
    )
    others = around(hidden)
    cq, sq = call(
        "queries",
        query_kernel,
        [X, X, VEC, VEC, WCOL, WCOL],
        [XCOL, XCOL],
        [shape(ROWS, D), shape(ROWS, D)],
        [pltpu.VMEM((ROWS, D), BF)],
        work=4 * ROWS * D * D,
    )(tokens, hidden, query_gain, query_shift, cross_query, self_query)
    self_state = call_part("self_own", [hidden], [], sq, self_key, self_value)
    *self_state, onward = lax.optimization_barrier((*self_state, onward))
    base = call_others(
        others, sq, self_key, self_value, self_output, self_state, tokens
    )

    mine = lax.all_to_all(onward, ROUTE, split_axis=0, concat_axis=0, tiled=True)
    cam_parts = [cam_own] + around(cam_own)
    mine, base, *cam_parts[1:] = lax.optimization_barrier((mine, base, *cam_parts[1:]))
    mine = from_tiles(mine)
    near_a = lax.ppermute(mine, "tok", turn(1))
    near_b = lax.ppermute(mine, "tok", turn(3))
    far_a = lax.ppermute(near_a[: ROWS // 2], "tok", turn(1))
    far_b = lax.ppermute(near_b[ROWS // 2 :], "tok", turn(3))
    cam_ctx = call(
        "camera_attention",
        camera_kernel,
        [CAMS] * 4 + [X, W, W],
        ALL,
        shape(D, ROWS, dtype=jnp.float32),
        steps=1,
        work=4 * 128 * D * D + 16 * ROWS * 128 * D,
    )(*cam_parts, cq, cross_key, cross_value)
    state = call_part("cross_own", [mine], [], cq, cross_key, cross_value)
    state = call_part("cross_near", [near_a, near_b], state, cq, cross_key, cross_value)
    return call_last(
        "cross_far",
        [far_a, far_b],
        [cam_ctx],
        (cq, cross_key, cross_value, cross_output),
        state,
        base,
    )


def solution(mesh):
    split = Mesh(mesh.devices.reshape(4, 2, 4, 2, 4), ("x", "zl", "zh", "core", "tok"))
    rows = P(("x", "zl", "zh", "core", "tok"), None)
    return jax.shard_map(
        local, mesh=split, in_specs=(rows,) + (P(),) * 16, out_specs=rows, check_vma=False
    )
```
